512 devices in a mesh: prompt: 32 (over z, y_lo), resp: 16 (over x, y_hi, core).
Axes of the slice: x: 4, y: 4 (y_hi: 2, y_lo: 2; y = y_hi * 2 + y_lo), z: 16, core: 2. Of those that a mesh axis runs over, the one named last changes fastest.
Arguments:
- queries: bfloat16 [65536, 1024], P(('prompt', 'resp')), may hold values from -6 to 6
- resp_kv: bfloat16 [65536, 256], P(('prompt', 'resp')), may hold values from -6 to 6
- prefix_kv: bfloat16 [65536, 256], P(('prompt', 'resp')), may hold values from -6 to 6
- upstream: bfloat16 [65536, 1024], P(('prompt', 'resp')), may hold values from -6 to 6
- gains: float32 [2, 128], replicated, may hold values from 0.5 to 1.5
- rewards: int32 [32, 16], P('prompt', 'resp'), may hold values from 0 to 3
- lengths: int32 [32], P('prompt'), may hold values from 256 to 2048, as said below
Outputs:
- grad_query: float32 [65536, 1024], P(('prompt', 'resp'))
- grad_response: float32 [65536, 256], P(('prompt', 'resp'))
- grad_prefix: float32 [65536, 256], P(('prompt', 'resp'))
- gain_grads: float32 [2, 128], replicated
The draws below stay inside these ranges and needn't reach their ends.
Inputs may be any that keep to these rules, and one draw needn't show every extreme that they name: `lengths`: at least one prompt has length 2048.
All inputs are finite; a program needn't handle non-finite values.
Results may differ from the reference program's by a relative error of at most 0.0069.
Values may be sent and summed in bfloat16 or wider, within the bound.
A program may use at most 64 MiB of HBM per device.

```python
import math
import jax
import jax.numpy as jnp
from jax import lax

HEAD = 128
GROUP_HEADS = 8
RESP_LEN = 128
RESPONSES = 16
PROMPTS = 32
PREFIX = 2048


def draw_lengths(key, part):
    key = jax.random.fold_in(key, 7)
    length_key, place_key = jax.random.split(key)
    drawn = jax.random.randint(length_key, (PROMPTS,), PREFIX // 8, PREFIX + 1)
    picked = jax.random.randint(place_key, (), 0, PROMPTS)
    chosen = jnp.where(jnp.arange(PROMPTS) == picked, PREFIX, drawn)
    return chosen.astype(jnp.int32)


def set_ends(result, rng, low, top_value):
    spot = [jax.random.randint(jax.random.fold_in(rng, axis), (), 0, length) for axis, length in enumerate(result.shape)]
    main_axis = result.shape.index(max(result.shape))
    beside = spot[:main_axis] + [(spot[main_axis] + 1) % result.shape[main_axis]] + spot[main_axis + 1:]
    return result.at[tuple(spot)].set(low).at[tuple(beside)].set(top_value)


def block_scale(stream_key, dims, shards, smallest, largest):
    def one(axis_at, shards_of):
        steps = jax.random.uniform(jax.random.fold_in(jax.random.fold_in(stream_key, 6), axis_at), (shards_of,), jnp.float32, smallest / len(shards), largest / len(shards))
        return jnp.repeat(jnp.exp(steps), dims[axis_at] // shards_of).reshape((-1,) + (1,) * (len(dims) - axis_at - 1))

    level = one(*shards[0])
    for cut in shards[1:]:
        level = level * one(*cut)
    return level


def normal_values(stream_key, extent, deviation, reach, shards=(), held_as=jnp.bfloat16):
    entries = deviation * jax.random.normal(stream_key, extent, jnp.float32)
    if shards:
        entries = entries * block_scale(stream_key, extent, shards, -0.22, 0.18)
    return jnp.clip(entries, -reach, reach).astype(held_as)


def setup_inputs(seed: int = 0) -> dict:
    seeds = jax.random.split(jax.random.key(seed), 8)
    queries = normal_values(seeds[0], (PROMPTS * RESPONSES * RESP_LEN, GROUP_HEADS * HEAD), 1.0, 6.0, ((0, 512),))
    resp_kv = normal_values(seeds[1], (PROMPTS * RESPONSES * RESP_LEN, 2 * HEAD), 1.0, 6.0, ((0, 512),))
    prefix_kv = normal_values(seeds[2], (PROMPTS * PREFIX, 2 * HEAD), 1.0, 6.0, ((0, 512),))
    upstream = normal_values(seeds[3], (PROMPTS * RESPONSES * RESP_LEN, GROUP_HEADS * HEAD), 1.0, 6.0, ((0, 512),))
    gains = jnp.clip(1.0 + 0.1 * jax.random.normal(seeds[4], (2, HEAD), jnp.float32), 0.5, 1.5)
    rewards = set_ends(jax.random.randint(seeds[5], (PROMPTS, RESPONSES), 0, 4), jax.random.fold_in(seeds[5], 1), 0, 3).astype(jnp.int32)
    lengths = draw_lengths(jax.random.fold_in(seeds[7], 71), 0)
    return {"queries": queries, "resp_kv": resp_kv, "prefix_kv": prefix_kv, "upstream": upstream, "gains": gains, "rewards": rewards, "lengths": lengths}


norm_eps = 1e-06

def half_round(values):
    return lax.optimization_barrier(values.astype(jnp.bfloat16))

def unit_scale(values):
    inverse = lax.rsqrt(lax.optimization_barrier(jnp.mean(values * values, axis=-1, keepdims=True)) + norm_eps)
    return (values * inverse, inverse)

def unit_back(grad_normed, unit_values, inverse, gain):
    grad_unit = grad_normed * gain
    inner = lax.optimization_barrier(jnp.mean(grad_unit * unit_values, axis=-1, keepdims=True))
    return inverse * (grad_unit - unit_values * inner)

def advantage_of(reward_total, squares, group_size, reward_value):
    spread = jnp.sqrt(group_size * squares - reward_total * reward_total) / group_size
    return (reward_value - reward_total / group_size) / jnp.maximum(spread, 1.0)

def response_grads(query_rows, pair_rows, upstream_rows, advantage, prefix_keys, prefix_values, visible, gains):
    score_scale = HEAD ** (-0.5)
    query_cube = query_rows.astype(jnp.float32).reshape(RESP_LEN, GROUP_HEADS, HEAD)
    query_unit, query_inverse = unit_scale(query_cube)
    query_half = half_round(query_unit * gains[0]).astype(jnp.float32)
    key_unit, key_inverse = unit_scale(pair_rows[:, :HEAD].astype(jnp.float32))
    key_half = half_round(key_unit * gains[1])
    all_keys = jnp.concatenate([prefix_keys, key_half], axis=0).astype(jnp.float32)
    all_values = jnp.concatenate([prefix_values, pair_rows[:, HEAD:]], axis=0).astype(jnp.float32)
    positions = jnp.arange(RESP_LEN)
    causal = (positions[:, None] >= positions[None, :]).astype(jnp.float32)
    shown = jnp.broadcast_to(visible.astype(jnp.float32)[None, :], (RESP_LEN, PREFIX))
    mask_rows = jnp.concatenate([shown, causal], axis=1)
    scores = jnp.einsum('thd,jd->thj', query_half, all_keys) * score_scale
    weights = jnp.exp(scores) * mask_rows[:, None, :]
    denominator = lax.optimization_barrier(jnp.sum(weights, axis=-1))
    numerator = jnp.einsum('thj,jd->thd', half_round(weights).astype(jnp.float32), all_values)
    output = numerator / denominator[..., None]
    grad_out = half_round(advantage * upstream_rows.astype(jnp.float32).reshape(RESP_LEN, GROUP_HEADS, HEAD)).astype(jnp.float32)
    delta_rows = lax.optimization_barrier(jnp.sum(grad_out * output, axis=-1))
    probs = weights / denominator[..., None]
    grad_probs = jnp.einsum('thd,jd->thj', grad_out, all_values)
    grad_scores = half_round(probs * (grad_probs - delta_rows[..., None]) * score_scale).astype(jnp.float32)
    grad_normed = jnp.einsum('thj,jd->thd', grad_scores, all_keys)
    grad_keys = jnp.einsum('thj,thd->jd', grad_scores, query_half)
    grad_values = jnp.einsum('thj,thd->jd', half_round(probs).astype(jnp.float32), grad_out)
    grad_query = unit_back(grad_normed, query_unit, query_inverse, gains[0]).reshape(RESP_LEN, GROUP_HEADS * HEAD)
    query_gain = lax.optimization_barrier(jnp.sum(grad_normed * query_unit, axis=(0, 1)))
    own_keys = grad_keys[PREFIX:]
    grad_pair = jnp.concatenate([unit_back(own_keys, key_unit, key_inverse, gains[1]), grad_values[PREFIX:]], axis=1)
    key_gain = lax.optimization_barrier(jnp.sum(own_keys * key_unit, axis=0))
    prefix_part = jnp.concatenate([grad_keys[:PREFIX], grad_values[:PREFIX]], axis=1)
    return (grad_query, grad_pair, prefix_part, jnp.stack([query_gain, key_gain]))

def reference(queries, resp_kv, prefix_kv, upstream, gains, rewards, lengths):

    def one_prompt(items):
        query_block, pair_block, prefix_block, upstream_block, reward_row, prompt_length = items
        prefix_unit, prefix_inverse = unit_scale(prefix_block[:, :HEAD].astype(jnp.float32))
        prefix_keys = half_round(prefix_unit * gains[1])
        prefix_values = prefix_block[:, HEAD:]
        visible = jnp.arange(PREFIX) < prompt_length
        reward_float = reward_row.astype(jnp.float32)
        advantages = advantage_of(jnp.sum(reward_float), jnp.sum(reward_float * reward_float), float(RESPONSES), reward_float)

        def one_response(inner_items):
            query_rows, pair_rows, upstream_rows, advantage = inner_items
            return response_grads(query_rows, pair_rows, upstream_rows, advantage, prefix_keys, prefix_values, visible, gains)
        grad_query, grad_pair, prefix_parts, gain_parts = lax.map(one_response, (query_block, pair_block, upstream_block, advantages))
        prefix_sum = lax.optimization_barrier(jnp.sum(prefix_parts, axis=0))
        prefix_grad = jnp.concatenate([unit_back(prefix_sum[:, :HEAD], prefix_unit, prefix_inverse, gains[1]), prefix_sum[:, HEAD:]], axis=1)
        key_prefix = lax.optimization_barrier(jnp.sum(prefix_sum[:, :HEAD] * prefix_unit, axis=0))
        gain_sum = lax.optimization_barrier(jnp.sum(gain_parts, axis=0)) + jnp.stack([jnp.zeros_like(key_prefix), key_prefix])
        return (grad_query, grad_pair, prefix_grad, gain_sum)
    inputs = (queries.reshape(PROMPTS, RESPONSES, RESP_LEN, GROUP_HEADS * HEAD), resp_kv.reshape(PROMPTS, RESPONSES, RESP_LEN, 2 * HEAD), prefix_kv.reshape(PROMPTS, PREFIX, 2 * HEAD), upstream.reshape(PROMPTS, RESPONSES, RESP_LEN, GROUP_HEADS * HEAD), rewards, lengths)
    grad_query, grad_pair, prefix_grad, gain_sum = lax.map(one_prompt, inputs)
    gain_grads = lax.optimization_barrier(jnp.sum(gain_sum, axis=0)) / math.sqrt(PROMPTS * RESPONSES * RESP_LEN)
    return (grad_query.reshape(PROMPTS * RESPONSES * RESP_LEN, GROUP_HEADS * HEAD), grad_pair.reshape(PROMPTS * RESPONSES * RESP_LEN, 2 * HEAD), prefix_grad.reshape(PROMPTS * PREFIX, 2 * HEAD), gain_grads)
```

```python
import functools
import math

import jax
import jax.numpy as jnp
from jax import lax
from jax.experimental import pallas as pl
from jax.experimental.pallas import tpu as pltpu
from jax.sharding import PartitionSpec as P

HEAD = 128
HEADS = 8
ROWS = 128
QUERIES = HEADS * ROWS
CHUNK = 256
EPS = 1e-06
SCALE = HEAD ** (-0.5)
EXP2 = SCALE * math.log2(math.e)
MESH = pl.DeviceIdType.MESH
F32 = jnp.float32
BF16 = jnp.bfloat16


def unit_scale(values):
    inverse = lax.rsqrt(jnp.mean(values * values, axis=-1, keepdims=True) + EPS)
    return values * inverse, inverse


def unit_back(grad_normed, unit_values, inverse, gain):
    grad_unit = grad_normed * gain
    inner = jnp.mean(grad_unit * unit_values, axis=-1, keepdims=True)
    return inverse * (grad_unit - unit_values * inner)


def fold(values):
    rows, columns = values.shape
    return jnp.sum(values.reshape(rows // 8, 8, columns), axis=0)


def mm(left, right):
    return lax.dot_general(left, right, (((1,), (0,)), ((), ())), preferred_element_type=F32)


def chunks():
    return [slice(start, start + CHUNK) for start in range(0, QUERIES, CHUNK)]


def heads():
    return [slice(h * HEAD, (h + 1) * HEAD) for h in range(HEADS)]


def kernel(
    sizes,
    queries,
    resp_kv,
    prefix_kv,
    upstream,
    gains,
    rewards,
    lengths,
    grad_query,
    grad_response,
    grad_prefix,
    gain_grads,
    q_in,
    u_in,
    r_in,
    kv,
    q_t,
    u_t,
    q_rows,
    u_rows,
    key_unit,
    key_half,
    weights,
    probes,
    den_sum,
    delta_sum,
    grads_t,
    key_gain,
    reward_in,
    pair_out,
    pair_in,
    part_out,
    part_in,
    gain_buf,
    in_sem,
    ag_send,
    ag_recv,
    relay_send,
    relay_recv,
    reward_send,
    reward_recv,
    pair_send,
    pair_recv,
    part_send,
    part_recv,
    gain_send,
    gain_recv,
):
    prompts, responses = sizes
    chips = responses // 2
    planes = prompts // 2
    prompt = lax.axis_index("prompt")
    resp = lax.axis_index("resp")
    chip = resp // 2
    core = lax.rem(resp, 2)
    low = lax.rem(prompt, 2)

    def to_chip(step):
        return (prompt, lax.rem(chip + step, chips) * 2 + core)

    sibling = (prompt, resp + 1 - 2 * core)

    def to_plane(step):
        row = lax.rem(low + step // chips, 2)
        return (prompt - low + row, lax.rem(chip + lax.rem(step, chips), chips) * 2 + core)

    def to_z(step):
        return (lax.rem(prompt + 2 * step, prompts), resp)

    barrier = pltpu.get_barrier_semaphore()

    def greet(device):
        pl.semaphore_signal(barrier, inc=1, device_id=device, device_id_type=MESH)

    copies = [
        pltpu.make_async_copy(prefix_kv, kv.at[0, 0], in_sem.at[0]),
        pltpu.make_async_copy(queries, q_in, in_sem.at[1]),
        pltpu.make_async_copy(upstream, u_in, in_sem.at[2]),
        pltpu.make_async_copy(resp_kv, r_in, in_sem.at[3]),
    ]
    for copy in copies:
        copy.start()
    greet(sibling)

    @pl.loop(1, 2 * chips)
    def _(step):
        greet(to_plane(step))

    @pl.loop(1, planes)
    def _(step):
        greet(to_z(step))

    copies[0].wait()
    pl.semaphore_wait(barrier, 1 + (2 * chips - 1) + (planes - 1))

    def remote(src, dst, send, recv, device):
        return pltpu.make_async_remote_copy(
            src_ref=src, dst_ref=dst, send_sem=send, recv_sem=recv, device_id=device, device_id_type=MESH
        )

    def gather(step):
        return remote(kv.at[0, 0], kv.at[chips - step, 0], ag_send.at[step], ag_recv.at[chips - step], to_chip(step))

    def relay(step):
        return remote(kv.at[step, 0], kv.at[step, 1], relay_send.at[step], relay_recv.at[step], sibling)

    def reward_copy(step):
        return remote(
            reward_in.at[0],
            reward_in.at[chips - step],
            reward_send.at[step],
            reward_recv.at[chips - step],
            to_chip(step),
        )

    @pl.loop(1, chips)
    def _(step):
        gather(step).start()

    relay(0).start()
    own_reward = rewards[0, 0].astype(F32)
    reward_in[chips] = jnp.full((8, 128), own_reward, F32)
    swap = remote(reward_in.at[chips], reward_in.at[chips + 1], reward_send.at[0], reward_recv.at[0], sibling)
    swap.start()

    gain_query = gains[0:1, :]
    gain_key = gains[1:2, :]
    length = lengths[0]

    for copy in copies[1:]:
        copy.wait()
    for h, part in enumerate(heads()):
        unit, _ = unit_scale(q_in[:, part].astype(F32))
        q_t[:, part] = jnp.transpose((unit * gain_query).astype(BF16))
        u_t[:, part] = jnp.transpose(u_in[:, part])
    den_sum[...] = jnp.zeros_like(den_sum)
    delta_sum[...] = jnp.zeros_like(delta_sum)
    key_gain[...] = jnp.zeros_like(key_gain)

    swap.wait()
    pair = reward_in[chips], reward_in[chips + 1]
    row = lax.broadcasted_iota(jnp.int32, (8, 128), 0)
    reward_in[0] = jnp.where(row == 0, pair[0] + pair[1], pair[0] * pair[0] + pair[1] * pair[1])

    @pl.loop(1, chips)
    def _(step):
        reward_copy(step).start()

    def forward(slot, key_rows, value_rows, mask_of):
        unit, _ = unit_scale(key_rows.astype(F32))
        key_unit[slot] = unit
        half = (unit * gain_key).astype(BF16)
        key_half[slot] = half
        for part in chunks():
            scores = mm(half, q_t[:, part])
            seen = jnp.where(mask_of(part), jnp.exp2(scores * EXP2), 0.0)
            probe = mm(value_rows, u_t[:, part])
            den_sum[:, part] += fold(seen)
            delta_sum[:, part] += fold(seen * probe)
            weights[slot, :, part] = seen
            probes[slot, :, part] = probe

    def prefix_forward(step, side):
        owner = lax.rem(chip + step, chips) * 2 + (core if side == 0 else 1 - core)
        place = lax.broadcasted_iota(jnp.int32, (ROWS, CHUNK), 0) + owner * ROWS
        visible = place < length
        forward(step * 2 + side, kv[step, side, :, :HEAD], kv[step, side, :, HEAD:], lambda part: visible)

    own_slot = 2 * chips
    key_place = lax.broadcasted_iota(jnp.int32, (ROWS, CHUNK), 0)
    token = lax.rem(lax.broadcasted_iota(jnp.int32, (ROWS, CHUNK), 1), ROWS)
    forward(own_slot, r_in[:, :HEAD], r_in[:, HEAD:], lambda part: key_place <= token)
    prefix_forward(0, 0)

    @pl.loop(1, chips)
    def _(step):
        gather(chips - step).wait_recv()
        relay(step).start()
        prefix_forward(step, 0)
        relay(step - 1).wait_recv()
        prefix_forward(step - 1, 1)

    relay(chips - 1).wait_recv()
    prefix_forward(chips - 1, 1)

    @pl.loop(1, chips)
    def _(step):
        reward_copy(chips - step).wait_recv()

    total = reward_in[0]
    for step in range(1, chips):
        total = total + reward_in[step]
    group = float(responses)
    reward_total, squares = total[0:1, 0:1], total[1:2, 0:1]
    spread = jnp.sqrt(group * squares - reward_total * reward_total) / group
    advantage = (own_reward - reward_total / group) / jnp.maximum(spread, 1.0)

    inverse_den = 1.0 / jnp.sum(den_sum[...], axis=0, keepdims=True)
    delta = jnp.sum(delta_sum[...], axis=0, keepdims=True) * inverse_den
    delta_sum[0:1, :] = delta
    value_factor = inverse_den * advantage
    key_factor = value_factor * SCALE
    den_sum[0:1, :] = key_factor
    for part in heads():
        q_rows[part, :] = jnp.transpose((q_t[:, part].astype(F32) * key_factor[:, part]).astype(BF16))
        u_rows[part, :] = jnp.transpose((u_t[:, part].astype(F32) * value_factor[:, part]).astype(BF16))
    grads_t[...] = jnp.zeros_like(grads_t)

    def backward(slot):
        keys_t = jnp.transpose(key_half[slot])
        grad_key = jnp.zeros((ROWS, HEAD), F32)
        grad_value = jnp.zeros((ROWS, HEAD), F32)
        for part in chunks():
            seen = weights[slot, :, part]
            score = (seen * (probes[slot, :, part] - delta_sum[0:1, part])).astype(BF16)
            grad_key += mm(score, q_rows[part, :])
            grad_value += mm(seen.astype(BF16), u_rows[part, :])
            grads_t[:, part] += mm(keys_t, score)
        key_gain[...] += fold(grad_key * key_unit[slot])
        return grad_key, grad_value

    def pair_copy(step):
        return remote(pair_out.at[step], pair_in.at[step], pair_send.at[step], pair_recv.at[step], sibling)

    def part_copy(step):
        return remote(
            part_out.at[step], part_in.at[chips - step], part_send.at[step], part_recv.at[chips - step], to_chip(step)
        )

    def prefix_backward(step):
        grad_key, grad_value = backward(step * 2 + 1)
        pair_out[step, :, :HEAD] = grad_key.astype(BF16)
        pair_out[step, :, HEAD:] = grad_value.astype(BF16)
        pair_copy(step).start()
        return backward(step * 2)

    @pl.loop(1, chips)
    def _(step):
        grad_key, grad_value = prefix_backward(step)
        pair_copy(step).wait_recv()
        part_out[step, :, :HEAD] = (grad_key + pair_in[step, :, :HEAD].astype(F32)).astype(BF16)
        part_out[step, :, HEAD:] = (grad_value + pair_in[step, :, HEAD:].astype(F32)).astype(BF16)
        part_copy(step).start()

    sum_key, sum_value = prefix_backward(0)
    self_key, self_value = backward(own_slot)

    query_gain = jnp.zeros((8, HEAD), F32)
    key_factor = den_sum[0:1, :]
    for part in heads():
        grad_normed = jnp.transpose(grads_t[:, part] * key_factor[:, part])
        unit, inverse = unit_scale(q_in[:, part].astype(F32))
        query_gain += fold(grad_normed * unit)
        grad_query[:, part] = unit_back(grad_normed, unit, inverse, gain_query)

    first = 1
    plane_base = 2
    z_base = plane_base + 2 * chips
    z_own = z_base + planes

    def gain_core():
        return remote(gain_buf.at[0], gain_buf.at[first], gain_send.at[first], gain_recv.at[first], sibling)

    def gain_plane(step):
        back = lax.rem(chips - lax.rem(step, chips), chips) + (step // chips) * chips
        return remote(
            gain_buf.at[plane_base],
            gain_buf.at[plane_base + back],
            gain_send.at[plane_base + step],
            gain_recv.at[plane_base + back],
            to_plane(step),
        )

    def gain_z(step):
        return remote(
            gain_buf.at[z_own],
            gain_buf.at[z_base + planes - step],
            gain_send.at[z_base + step],
            gain_recv.at[z_base + planes - step],
            to_z(step),
        )

    def spread_rows(query_row, key_row):
        return jnp.where(row == 0, query_row, jnp.where(row == 1, key_row, 0.0))

    gain_buf[0] = spread_rows(
        jnp.sum(query_gain, axis=0, keepdims=True), jnp.sum(key_gain[...], axis=0, keepdims=True)
    )
    gain_core().start()

    unit, inverse = unit_scale(r_in[:, :HEAD].astype(F32))
    grad_response[:, :HEAD] = unit_back(self_key, unit, inverse, gain_key)
    grad_response[:, HEAD:] = self_value

    gain_core().wait_recv()
    gain_buf[plane_base] = gain_buf[0] + gain_buf[first]

    @pl.loop(1, 2 * chips)
    def _(step):
        gain_plane(step).start()

    pair_copy(0).wait_recv()
    sum_key += pair_in[0, :, :HEAD].astype(F32)
    sum_value += pair_in[0, :, HEAD:].astype(F32)
    for step in range(1, chips):
        part_copy(chips - step).wait_recv()
        sum_key += part_in[step, :, :HEAD].astype(F32)
        sum_value += part_in[step, :, HEAD:].astype(F32)
    unit, inverse = unit_scale(kv[0, 0, :, :HEAD].astype(F32))
    grad_prefix[:, :HEAD] = unit_back(sum_key, unit, inverse, gain_key)
    grad_prefix[:, HEAD:] = sum_value

    @pl.loop(1, 2 * chips)
    def _(step):
        gain_plane(step).wait_recv()

    total = gain_buf[plane_base]
    for step in range(1, 2 * chips):
        total = total + gain_buf[plane_base + step]
    gain_buf[z_own] = total

    @pl.loop(1, planes)
    def _(step):
        gain_z(step).start()

    @pl.loop(1, planes)
    def _(step):
        gain_z(step).wait_recv()

    total = gain_buf[z_own]
    for step in range(1, planes):
        total = total + gain_buf[z_base + step]
    gain_grads[...] = total[0:2, :] / math.sqrt(prompts * responses * ROWS)

    relay(0).wait_send()
    pair_copy(0).wait_send()
    gain_core().wait_send()

    @pl.loop(1, chips)
    def _(step):
        gather(step).wait_send()
        relay(step).wait_send()
        reward_copy(step).wait_send()
        pair_copy(step).wait_send()
        part_copy(step).wait_send()

    @pl.loop(1, 2 * chips)
    def _(step):
        gain_plane(step).wait_send()

    @pl.loop(1, planes)
    def _(step):
        gain_z(step).wait_send()


def local(queries, resp_kv, prefix_kv, upstream, gains, rewards, lengths):
    prompts, responses = lax.axis_size("prompt"), lax.axis_size("resp")
    chips, planes = responses // 2, prompts // 2
    slots = responses + 1
    gain_slots = 2 + 2 * chips + planes + 1
    vmem = pl.BlockSpec(memory_space=pltpu.VMEM)
    smem = pl.BlockSpec(memory_space=pltpu.SMEM)
    hbm = pl.BlockSpec(memory_space=pl.ANY)
    dma = pltpu.SemaphoreType.DMA
    return pl.pallas_call(
        functools.partial(kernel, (prompts, responses)),
        out_shape=(
            jax.ShapeDtypeStruct((ROWS, QUERIES), F32),
            jax.ShapeDtypeStruct((ROWS, 2 * HEAD), F32),
            jax.ShapeDtypeStruct((ROWS, 2 * HEAD), F32),
            jax.ShapeDtypeStruct((2, HEAD), F32),
        ),
        in_specs=[hbm, hbm, hbm, hbm, vmem, smem, smem],
        out_specs=(vmem, vmem, vmem, vmem),
        scratch_shapes=[
            pltpu.VMEM((ROWS, QUERIES), BF16),
            pltpu.VMEM((ROWS, QUERIES), BF16),
            pltpu.VMEM((ROWS, 2 * HEAD), BF16),
            pltpu.VMEM((chips, 2, ROWS, 2 * HEAD), BF16),
            pltpu.VMEM((HEAD, QUERIES), BF16),
            pltpu.VMEM((HEAD, QUERIES), BF16),
            pltpu.VMEM((QUERIES, HEAD), BF16),
            pltpu.VMEM((QUERIES, HEAD), BF16),
            pltpu.VMEM((slots, ROWS, HEAD), F32),
            pltpu.VMEM((slots, ROWS, HEAD), BF16),
            pltpu.VMEM((slots, ROWS, QUERIES), F32),
            pltpu.VMEM((slots, ROWS, QUERIES), F32),
            pltpu.VMEM((8, QUERIES), F32),
            pltpu.VMEM((8, QUERIES), F32),
            pltpu.VMEM((HEAD, QUERIES), F32),
            pltpu.VMEM((8, HEAD), F32),
            pltpu.VMEM((chips + 2, 8, 128), F32),
            pltpu.VMEM((chips, ROWS, 2 * HEAD), BF16),
            pltpu.VMEM((chips, ROWS, 2 * HEAD), BF16),
            pltpu.VMEM((chips, ROWS, 2 * HEAD), BF16),
            pltpu.VMEM((chips, ROWS, 2 * HEAD), BF16),
            pltpu.VMEM((gain_slots, 8, HEAD), F32),
            dma((4,)),
            dma((chips,)),
            dma((chips,)),
            dma((chips,)),
            dma((chips,)),
            dma((chips,)),
            dma((chips,)),
            dma((chips,)),
            dma((chips,)),
            dma((chips,)),
            dma((chips,)),
            dma((gain_slots,)),
            dma((gain_slots,)),
        ],
        compiler_params=pltpu.CompilerParams(
            collective_id=0, has_side_effects=True, vmem_limit_bytes=48 * 1024 * 1024
        ),
    )(queries, resp_kv, prefix_kv, upstream, gains, rewards, lengths)


def solution(mesh):
    rows = P(("prompt", "resp"), None)
    return jax.shard_map(
        local,
        mesh=mesh,
        in_specs=(rows, rows, rows, rows, P(), P("prompt", "resp"), P("prompt")),
        out_specs=(rows, rows, rows, P()),
        check_vma=False,
    )
```

```python
import functools
import math

import jax
import jax.numpy as jnp
from jax import lax
from jax.experimental import pallas as pl
from jax.experimental.pallas import tpu as pltpu
from jax.sharding import PartitionSpec as P

HEAD = 128
HEADS = 8
ROWS = 128
QUERIES = HEADS * ROWS
CHUNK = 256
BLOCKS = 4
VMEM_LIMIT = 63 * 1024 * 1024
EPS = 1e-06
SCALE = HEAD ** (-0.5)
EXP2 = SCALE * math.log2(math.e)
MESH = pl.DeviceIdType.MESH
F32 = jnp.float32
BF16 = jnp.bfloat16


def unit_scale(values):
    inverse = lax.rsqrt(jnp.mean(values * values, axis=-1, keepdims=True) + EPS)
    return values * inverse, inverse


def unit_back(grad_normed, unit_values, inverse, gain):
    grad_unit = grad_normed * gain
    inner = jnp.mean(grad_unit * unit_values, axis=-1, keepdims=True)
    return inverse * (grad_unit - unit_values * inner)


def fold(values):
    rows, columns = values.shape
    return jnp.sum(values.reshape(rows // 8, 8, columns), axis=0)


def mm(left, right):
    return lax.dot_general(left, right, (((1,), (0,)), ((), ())), preferred_element_type=F32)


def chunks():
    return [slice(start, start + CHUNK) for start in range(0, QUERIES, CHUNK)]


def heads():
    return [slice(h * HEAD, (h + 1) * HEAD) for h in range(HEADS)]


def kernel(
    sizes,
    queries,
    resp_kv,
    prefix_kv,
    upstream,
    gains,
    rewards,
    lengths,
    grad_query,
    grad_response,
    grad_prefix,
    gain_grads,
    q_in,
    u_in,
    r_in,
    g_in,
    reward_word,
    length_word,
    kv,
    unit_t,
    q_t,
    u_t,
    key_rows,
    value_rows,
    weights,
    marks,
    den_sum,
    mark_sum,
    base,
    mark_grads,
    weight_grads,
    reward_in,
    pair_out,
    pair_in,
    part_out,
    part_in,
    gain_buf,
    query_out,
    response_out,
    prefix_out,
    gain_out,
    in_sem,
    out_sem,
    ag_send,
    ag_recv,
    relay_send,
    relay_recv,
    reward_send,
    reward_recv,
    pair_send,
    pair_recv,
    part_send,
    part_recv,
    gain_send,
    gain_recv,
):
    prompts, responses = sizes
    chips = responses // 2
    planes = prompts // 2
    prompt = lax.axis_index("prompt")
    resp = lax.axis_index("resp")
    chip = resp // 2
    core = lax.rem(resp, 2)
    low = lax.rem(prompt, 2)

    def to_chip(step):
        return (prompt, lax.rem(chip + step, chips) * 2 + core)

    sibling = (prompt, resp + 1 - 2 * core)

    def to_plane(step):
        row = lax.rem(low + step // chips, 2)
        return (prompt - low + row, lax.rem(chip + lax.rem(step, chips), chips) * 2 + core)

    def to_z(step):
        return (lax.rem(prompt + 2 * step, prompts), resp)

    barrier = pltpu.get_barrier_semaphore()

    def greet(device):
        pl.semaphore_signal(barrier, inc=1, device_id=device, device_id_type=MESH)

    copies = [
        pltpu.make_async_copy(prefix_kv, kv.at[0, 0], in_sem.at[0]),
        pltpu.make_async_copy(queries, q_in, in_sem.at[1]),
        pltpu.make_async_copy(upstream, u_in, in_sem.at[2]),
        pltpu.make_async_copy(resp_kv, r_in, in_sem.at[3]),
        pltpu.make_async_copy(gains, g_in, in_sem.at[4]),
        pltpu.make_async_copy(rewards, reward_word, in_sem.at[5]),
        pltpu.make_async_copy(lengths, length_word, in_sem.at[6]),
    ]
    for copy in copies:
        copy.start()

    @pl.loop(1, planes)
    def _(step):
        greet(to_z(step))

    @pl.loop(1, 2 * chips)
    def _(step):
        greet(to_plane(step))

    greet(sibling)

    copies[0].wait()
    pl.semaphore_wait(barrier, 1 + (2 * chips - 1) + (planes - 1))

    def remote(src, dst, send, recv, device):
        return pltpu.make_async_remote_copy(
            src_ref=src, dst_ref=dst, send_sem=send, recv_sem=recv, device_id=device, device_id_type=MESH
        )

    def gather(step):
        return remote(kv.at[0, 0], kv.at[0, chips - step], ag_send.at[step], ag_recv.at[chips - step], to_chip(step))

    def relay(step):
        return remote(kv.at[0, step], kv.at[1, step], relay_send.at[step], relay_recv.at[step], sibling)

    def reward_copy(step):
        return remote(
            reward_in.at[0],
            reward_in.at[chips - step],
            reward_send.at[step],
            reward_recv.at[chips - step],
            to_chip(step),
        )

    @pl.loop(1, chips)
    def _(step):
        gather(step).start()

    relay(0).start()
    for copy in copies[1:]:
        copy.wait()
    own_reward = reward_word[0, 0].astype(F32)
    reward_in[chips] = jnp.full((8, 128), own_reward, F32)
    swap = remote(reward_in.at[chips], reward_in.at[chips + 1], reward_send.at[0], reward_recv.at[0], sibling)
    swap.start()

    gain_query = g_in[0:1, :]
    gain_key = g_in[1:2, :]
    length = length_word[0]

    for part in heads():
        unit, _ = unit_scale(q_in[:, part].astype(F32))
        unit_t[:, part] = jnp.transpose(unit)
        q_t[:, part] = jnp.transpose((unit * gain_query).astype(BF16))
        u_t[:, part] = jnp.transpose(u_in[:, part])
    mark_grads[...] = jnp.zeros_like(mark_grads)
    weight_grads[...] = jnp.zeros_like(weight_grads)

    swap.wait()
    pair = reward_in[chips], reward_in[chips + 1]
    row = lax.broadcasted_iota(jnp.int32, (8, 128), 0)
    reward_in[0] = jnp.where(row == 0, pair[0] + pair[1], pair[0] * pair[0] + pair[1] * pair[1])

    @pl.loop(1, chips)
    def _(step):
        reward_copy(step).start()

    own_slot = 2 * chips

    def half_of(rows):
        unit, _ = unit_scale(rows.astype(F32))
        return (unit * gain_key).astype(BF16)

    def scores_of(half, rows, part, seen):
        weight = jnp.where(seen, jnp.exp2(mm(half, q_t[:, part]) * EXP2), 0.0)
        return weight, mm(rows, u_t[:, part])

    def visible(side, step):
        owner = lax.rem(chip + step, chips) * 2 + (core if side == 0 else 1 - core)
        return lax.broadcasted_iota(jnp.int32, (ROWS, CHUNK), 0) + owner * ROWS < length

    def collect(slots, keys_t, part):
        mark = jnp.concatenate([marks[slot, :, part] for slot in slots], axis=0)
        weight = jnp.concatenate([weights[slot, :, part] for slot in slots], axis=0)
        mark_grads[:, part] += mm(keys_t, mark)
        weight_grads[:, part] += mm(keys_t, weight)

    key_place = lax.broadcasted_iota(jnp.int32, (ROWS, CHUNK), 0)
    token = lax.rem(lax.broadcasted_iota(jnp.int32, (ROWS, CHUNK), 1), ROWS)
    first_keys = [half_of(r_in[:, :HEAD]), half_of(kv[0, 0, :, :HEAD])]
    first_values = [r_in[:, HEAD:], kv[0, 0, :, HEAD:]]
    first_seen = [key_place <= token, visible(0, 0)]
    first_slots = [own_slot, 0]
    first_t = jnp.transpose(jnp.concatenate(first_keys, axis=0))
    for part in chunks():
        found = [scores_of(half, rows, part, seen) for half, rows, seen in zip(first_keys, first_values, first_seen)]
        den = fold(found[0][0]) + fold(found[1][0])
        mean = jnp.sum(fold(found[0][0] * found[0][1]) + fold(found[1][0] * found[1][1]), axis=0, keepdims=True)
        mean = mean / jnp.sum(den, axis=0, keepdims=True)
        base[0:1, part] = mean
        den_sum[:, part] = den
        mark_total = jnp.zeros_like(den)
        for slot, (weight, probe) in zip(first_slots, found):
            mark = weight * (probe - mean)
            mark_total += fold(mark)
            weights[slot, :, part] = weight.astype(BF16)
            marks[slot, :, part] = mark.astype(BF16)
        mark_sum[:, part] = mark_total
        collect(first_slots, first_t, part)

    def forward(places):
        slots = [side * chips + step for side, step in places]
        keys = [half_of(kv[side, step, :, :HEAD]) for side, step in places]
        keys_t = jnp.transpose(jnp.concatenate(keys, axis=0))
        seen = [visible(side, step) for side, step in places]
        for part in chunks():
            for slot, half, mask, (side, step) in zip(slots, keys, seen, places):
                weight, probe = scores_of(half, kv[side, step, :, HEAD:], part, mask)
                mark = weight * (probe - base[0:1, part])
                den_sum[:, part] += fold(weight)
                mark_sum[:, part] += fold(mark)
                weights[slot, :, part] = weight.astype(BF16)
                marks[slot, :, part] = mark.astype(BF16)
        for part in chunks():
            collect(slots, keys_t, part)

    @pl.loop(1, chips)
    def _(step):
        gather(chips - step).wait_recv()
        relay(step).start()
        relay(step - 1).wait_recv()
        forward([(0, step), (1, step - 1)])

    relay(chips - 1).wait_recv()
    forward([(1, chips - 1)])

    @pl.loop(1, chips)
    def _(step):
        reward_copy(chips - step).wait_recv()

    total = reward_in[0]
    for step in range(1, chips):
        total = total + reward_in[step]
    group = float(responses)
    reward_total, squares = total[0:1, 0:1], total[1:2, 0:1]
    spread = jnp.sqrt(group * squares - reward_total * reward_total) / group
    advantage = (own_reward - reward_total / group) / jnp.maximum(spread, 1.0)

    inverse_den = 1.0 / jnp.sum(den_sum[...], axis=0, keepdims=True)
    delta = jnp.sum(mark_sum[...], axis=0, keepdims=True) * inverse_den
    value_factor = inverse_den * advantage
    key_factor = value_factor * SCALE

    plane_base = 2
    z_base = plane_base + 2 * chips
    z_own = z_base + planes

    def gain_core():
        return remote(gain_buf.at[0], gain_buf.at[1], gain_send.at[1], gain_recv.at[1], sibling)

    def gain_plane(step):
        back = lax.rem(chips - lax.rem(step, chips), chips) + (step // chips) * chips
        return remote(
            gain_buf.at[plane_base],
            gain_buf.at[plane_base + back],
            gain_send.at[plane_base + step],
            gain_recv.at[plane_base + back],
            to_plane(step),
        )

    def gain_z(step):
        return remote(
            gain_buf.at[z_own],
            gain_buf.at[z_base + planes - step],
            gain_send.at[z_base + step],
            gain_recv.at[z_base + planes - step],
            to_z(step),
        )

    query_total = jnp.zeros((HEAD, ROWS), F32)
    key_total = jnp.zeros((HEAD, ROWS), F32)
    for part in heads():
        grad_t = (mark_grads[:, part] - weight_grads[:, part] * delta[:, part]) * key_factor[:, part]
        mark_grads[:, part] = grad_t
        query_total += grad_t * unit_t[:, part]
        key_total += grad_t * q_t[:, part].astype(F32)
    query_row = jnp.sum(fold(jnp.transpose(query_total)), axis=0, keepdims=True)
    key_row = jnp.sum(fold(jnp.transpose(key_total)), axis=0, keepdims=True) / gain_key
    gain_buf[0] = jnp.where(row == 0, query_row, jnp.where(row == 1, key_row, 0.0))
    gain_core().start()

    for part in heads():
        scaled = q_t[:, part].astype(F32) * key_factor[:, part]
        key_rows[part, :] = jnp.transpose(scaled.astype(BF16))
        value_rows[part, :HEAD] = jnp.transpose((scaled * -delta[:, part]).astype(BF16))
        value_rows[part, HEAD:] = jnp.transpose((u_t[:, part].astype(F32) * value_factor[:, part]).astype(BF16))

    def backward(slot, count):
        mark = marks[pl.ds(slot, count)].reshape(count * ROWS, QUERIES)
        weight = weights[pl.ds(slot, count)].reshape(count * ROWS, QUERIES)
        both = mm(weight, value_rows[...])
        grad_key = both[:, :HEAD] + mm(mark, key_rows[...])
        return grad_key.reshape(count, ROWS, HEAD), both[:, HEAD:].reshape(count, ROWS, HEAD)

    def pair_copy(step):
        return remote(pair_out.at[step], pair_in.at[step], pair_send.at[step], pair_recv.at[step], sibling)

    def part_copy(step):
        return remote(
            part_out.at[step], part_in.at[chips - step], part_send.at[step], part_recv.at[chips - step], to_chip(step)
        )

    def join(step, grad_key, grad_value):
        pair_copy(step).wait_recv()
        grad_key += pair_in[step, :, :HEAD].astype(F32)
        grad_value += pair_in[step, :, HEAD:].astype(F32)
        return grad_key, grad_value

    def odd(first):
        grad_key, grad_value = backward(chips + first, BLOCKS)
        for at in range(BLOCKS):
            pair_out[first + at, :, :HEAD] = grad_key[at].astype(BF16)
            pair_out[first + at, :, HEAD:] = grad_value[at].astype(BF16)
            pair_copy(first + at).start()

    def even(first):
        grad_key, grad_value = backward(first, BLOCKS)
        for at in reversed(range(BLOCKS)):
            step = first + at
            sums = join(step, grad_key[at], grad_value[at])
            if step == 0:
                return sums
            part_out[step, :, :HEAD] = sums[0].astype(BF16)
            part_out[step, :, HEAD:] = sums[1].astype(BF16)
            part_copy(step).start()

    firsts = list(range(chips - BLOCKS, -1, -BLOCKS))
    for first in firsts:
        odd(first)
        if first == firsts[0]:
            gain_core().wait_recv()
            gain_buf[plane_base] = gain_buf[0] + gain_buf[1]

            @pl.loop(1, 2 * chips)
            def _(step):
                gain_plane(step).start()

        sums = even(first)
    sum_key, sum_value = sums
    self_key, self_value = backward(own_slot, 1)

    unit, inverse = unit_scale(r_in[:, :HEAD].astype(F32))
    response_out[:, :HEAD] = unit_back(self_key[0], unit, inverse, gain_key)
    response_out[:, HEAD:] = self_value[0]
    for part in heads():
        grad_normed = jnp.transpose(mark_grads[:, part])
        unit, inverse = unit_scale(q_in[:, part].astype(F32))
        query_out[:, part] = unit_back(grad_normed, unit, inverse, gain_query)
    out_copies = [
        pltpu.make_async_copy(query_out, grad_query, out_sem.at[0]),
        pltpu.make_async_copy(response_out, grad_response, out_sem.at[1]),
        pltpu.make_async_copy(prefix_out, grad_prefix, out_sem.at[2]),
        pltpu.make_async_copy(gain_out, gain_grads, out_sem.at[3]),
    ]
    out_copies[0].start()
    out_copies[1].start()

    @pl.loop(1, 2 * chips)
    def _(step):
        gain_plane(step).wait_recv()

    total = gain_buf[plane_base]
    for step in range(1, 2 * chips):
        total = total + gain_buf[plane_base + step]
    gain_buf[z_own] = total

    @pl.loop(1, planes)
    def _(step):
        gain_z(step).start()

    for step in range(1, chips):
        part_copy(chips - step).wait_recv()
        sum_key += part_in[step, :, :HEAD].astype(F32)
        sum_value += part_in[step, :, HEAD:].astype(F32)
    unit, inverse = unit_scale(kv[0, 0, :, :HEAD].astype(F32))
    prefix_out[:, :HEAD] = unit_back(sum_key, unit, inverse, gain_key)
    prefix_out[:, HEAD:] = sum_value
    out_copies[2].start()

    relay(0).wait_send()
    pair_copy(0).wait_send()
    gain_core().wait_send()

    @pl.loop(1, chips)
    def _(step):
        gather(step).wait_send()
        relay(step).wait_send()
        reward_copy(step).wait_send()
        pair_copy(step).wait_send()
        part_copy(step).wait_send()

    @pl.loop(1, 2 * chips)
    def _(step):
        gain_plane(step).wait_send()

    @pl.loop(1, planes)
    def _(step):
        gain_z(step).wait_recv()

    total = gain_buf[z_own]
    for step in range(1, planes):
        total = total + gain_buf[z_base + step]
    gain_out[...] = total[0:2, :] / math.sqrt(prompts * responses * ROWS)
    out_copies[3].start()

    @pl.loop(1, planes)
    def _(step):
        gain_z(step).wait_send()

    for copy in out_copies:
        copy.wait()


def hand_on(*refs):
    half = len(refs) // 2
    for taken, given in zip(refs[:half], refs[half:]):
        given[...] = taken[...]


def local(queries, resp_kv, prefix_kv, upstream, gains, rewards, lengths):
    prompts, responses = lax.axis_size("prompt"), lax.axis_size("resp")
    chips, planes = responses // 2, prompts // 2
    slots = responses + 1
    gain_slots = 2 + 2 * chips + planes + 1
    hbm = pl.BlockSpec(memory_space=pltpu.HBM)
    vmem = pl.BlockSpec(memory_space=pltpu.VMEM)
    dma = pltpu.SemaphoreType.DMA
    shapes = (
        jax.ShapeDtypeStruct((ROWS, QUERIES), F32),
        jax.ShapeDtypeStruct((ROWS, 2 * HEAD), F32),
        jax.ShapeDtypeStruct((ROWS, 2 * HEAD), F32),
        jax.ShapeDtypeStruct((2, HEAD), F32),
    )
    found = pl.pallas_call(
        functools.partial(kernel, (prompts, responses)),
        out_shape=shapes,
        in_specs=[hbm] * 7,
        out_specs=(hbm,) * 4,
        scratch_shapes=[
            pltpu.VMEM((ROWS, QUERIES), BF16),
            pltpu.VMEM((ROWS, QUERIES), BF16),
            pltpu.VMEM((ROWS, 2 * HEAD), BF16),
            pltpu.VMEM((2, HEAD), F32),
            pltpu.SMEM((1, 1), jnp.int32),
            pltpu.SMEM((1,), jnp.int32),
            pltpu.VMEM((2, chips, ROWS, 2 * HEAD), BF16),
            pltpu.VMEM((HEAD, QUERIES), F32),
            pltpu.VMEM((HEAD, QUERIES), BF16),
            pltpu.VMEM((HEAD, QUERIES), BF16),
            pltpu.VMEM((QUERIES, HEAD), BF16),
            pltpu.VMEM((QUERIES, 2 * HEAD), BF16),
            pltpu.VMEM((slots, ROWS, QUERIES), BF16),
            pltpu.VMEM((slots, ROWS, QUERIES), BF16),
            pltpu.VMEM((8, QUERIES), F32),
            pltpu.VMEM((8, QUERIES), F32),
            pltpu.VMEM((8, QUERIES), F32),
            pltpu.VMEM((HEAD, QUERIES), F32),
            pltpu.VMEM((HEAD, QUERIES), F32),
            pltpu.VMEM((chips + 2, 8, 128), F32),
            pltpu.VMEM((chips, ROWS, 2 * HEAD), BF16),
            pltpu.VMEM((chips, ROWS, 2 * HEAD), BF16),
            pltpu.VMEM((chips, ROWS, 2 * HEAD), BF16),
            pltpu.VMEM((chips, ROWS, 2 * HEAD), BF16),
            pltpu.VMEM((gain_slots, 8, HEAD), F32),
            pltpu.VMEM((ROWS, QUERIES), F32),
            pltpu.VMEM((ROWS, 2 * HEAD), F32),
            pltpu.VMEM((ROWS, 2 * HEAD), F32),
            pltpu.VMEM((2, HEAD), F32),
            dma((7,)),
            dma((4,)),
            dma((chips,)),
            dma((chips,)),
            dma((chips,)),
            dma((chips,)),
            dma((chips,)),
            dma((chips,)),
            dma((chips,)),
            dma((chips,)),
            dma((chips,)),
            dma((chips,)),
            dma((gain_slots,)),
            dma((gain_slots,)),
        ],
        compiler_params=pltpu.CompilerParams(
            collective_id=0, has_side_effects=True, vmem_limit_bytes=VMEM_LIMIT
        ),
    )(queries, resp_kv, prefix_kv, upstream, gains, rewards, lengths)
    return pl.pallas_call(
        hand_on,
        out_shape=shapes,
        in_specs=[vmem] * 4,
        out_specs=(vmem,) * 4,
        compiler_params=pltpu.CompilerParams(vmem_limit_bytes=VMEM_LIMIT),
    )(*found)


def solution(mesh):
    rows = P(("prompt", "resp"), None)
    return jax.shard_map(
        local,
        mesh=mesh,
        in_specs=(rows, rows, rows, rows, P(), P("prompt", "resp"), P("prompt")),
        out_specs=(rows, rows, rows, P()),
        check_vma=False,
    )
```

```python
import functools
import math

import jax
import jax.numpy as jnp
from jax import lax
from jax.experimental import pallas as pl
from jax.experimental.pallas import tpu as pltpu
from jax.sharding import PartitionSpec as P

HEAD = 128
HEADS = 8
ROWS = 128
QUERIES = HEADS * ROWS
CHUNK = 256
VMEM_LIMIT = 63 * 1024 * 1024
EPS = 1e-06
SCALE = HEAD ** (-0.5)
EXP2 = SCALE * math.log2(math.e)
MESH = pl.DeviceIdType.MESH
F32 = jnp.float32
BF16 = jnp.bfloat16


def unit_scale(values):
    inverse = lax.rsqrt(jnp.mean(values * values, axis=-1, keepdims=True) + EPS)
    return values * inverse, inverse


def unit_back(grad_normed, unit_values, inverse, gain):
    grad_unit = grad_normed * gain
    inner = jnp.mean(grad_unit * unit_values, axis=-1, keepdims=True)
    return inverse * (grad_unit - unit_values * inner)


def fold(values):
    rows, columns = values.shape
    return jnp.sum(values.reshape(rows // 8, 8, columns), axis=0)


def mm(left, right):
    return lax.dot_general(left, right, (((1,), (0,)), ((), ())), preferred_element_type=F32)


def chunks():
    return [slice(start, start + CHUNK) for start in range(0, QUERIES, CHUNK)]


def heads():
    return [slice(h * HEAD, (h + 1) * HEAD) for h in range(HEADS)]


def kernel(
    sizes,
    queries,
    resp_kv,
    prefix_kv,
    upstream,
    gains,
    rewards,
    lengths,
    grad_query,
    grad_response,
    grad_prefix,
    gain_grads,
    q_in,
    u_in,
    r_in,
    g_in,
    reward_word,
    length_word,
    kv,
    q_t,
    u_t,
    key_rows,
    value_rows,
    weights,
    marks,
    self_weights,
    self_marks,
    den_sum,
    mark_sum,
    base,
    mark_grads,
    weight_grads,
    stat_out,
    stat_in,
    grad_in,
    reward_in,
    part_out,
    part_in,
    gain_buf,
    query_out,
    response_out,
    prefix_out,
    gain_out,
    in_sem,
    out_sem,
    ag_send,
    ag_recv,
    reward_send,
    reward_recv,
    part_send,
    part_recv,
    twin_send,
    twin_recv,
    gain_send,
    gain_recv,
):
    prompts, responses = sizes
    chips = responses // 2
    planes = prompts // 2
    prompt = lax.axis_index("prompt")
    resp = lax.axis_index("resp")
    chip = resp // 2
    core = lax.rem(resp, 2)
    low = lax.rem(prompt, 2)

    def to_chip(step):
        return (prompt, lax.rem(chip + step, chips) * 2 + core)

    sibling = (prompt, resp + 1 - 2 * core)

    def to_plane(step):
        row = lax.rem(low + step // chips, 2)
        return (prompt - low + row, lax.rem(chip + lax.rem(step, chips), chips) * 2 + core)

    def to_z(step):
        return (lax.rem(prompt + 2 * step, prompts), resp)

    barrier = pltpu.get_barrier_semaphore()

    def greet(device):
        pl.semaphore_signal(barrier, inc=1, device_id=device, device_id_type=MESH)

    copies = [
        pltpu.make_async_copy(prefix_kv, kv.at[0], in_sem.at[0]),
        pltpu.make_async_copy(queries, q_in, in_sem.at[1]),
        pltpu.make_async_copy(upstream, u_in, in_sem.at[2]),
        pltpu.make_async_copy(resp_kv, r_in, in_sem.at[3]),
        pltpu.make_async_copy(gains, g_in, in_sem.at[4]),
        pltpu.make_async_copy(rewards, reward_word, in_sem.at[5]),
        pltpu.make_async_copy(lengths, length_word, in_sem.at[6]),
    ]
    for copy in copies:
        copy.start()

    @pl.loop(1, planes)
    def _(step):
        greet(to_z(step))

    @pl.loop(1, 2 * chips)
    def _(step):
        greet(to_plane(step))

    greet(sibling)

    copies[0].wait()
    pl.semaphore_wait(barrier, 1 + (2 * chips - 1) + (planes - 1))

    def remote(src, dst, send, recv, device):
        return pltpu.make_async_remote_copy(
            src_ref=src, dst_ref=dst, send_sem=send, recv_sem=recv, device_id=device, device_id_type=MESH
        )

    def gather(step):
        return remote(kv.at[0], kv.at[chips - step], ag_send.at[step], ag_recv.at[chips - step], to_chip(step))

    def twin(place, src, dst):
        return remote(src, dst, twin_send.at[place], twin_recv.at[place], sibling)

    def reward_copy(step):
        return remote(
            reward_in.at[0],
            reward_in.at[chips - step],
            reward_send.at[step],
            reward_recv.at[chips - step],
            to_chip(step),
        )

    @pl.loop(1, chips)
    def _(step):
        gather(step).start()

    for copy in copies[1:]:
        copy.wait()
    own_reward = reward_word[0, 0].astype(F32)
    reward_in[chips] = jnp.full((8, 128), own_reward, F32)
    send_reward = twin(3, reward_in.at[chips], reward_in.at[chips + 1])
    send_reward.start()

    gain_query = g_in[0:1, :]
    gain_key = g_in[1:2, :]
    length = length_word[0]

    for part in heads():
        unit, _ = unit_scale(q_in[:, part].astype(F32))
        q_t[0, :, part] = jnp.transpose((unit * gain_query).astype(BF16))
        u_t[0, :, part] = jnp.transpose(u_in[:, part])
    send_q = twin(0, q_t.at[0], q_t.at[1])
    send_u = twin(1, u_t.at[0], u_t.at[1])
    send_q.start()
    send_u.start()
    mark_grads[...] = jnp.zeros_like(mark_grads)
    weight_grads[...] = jnp.zeros_like(weight_grads)
    den_sum[1] = jnp.zeros_like(den_sum[1])
    mark_sum[1] = jnp.zeros_like(mark_sum[1])

    def half_of(rows):
        unit, _ = unit_scale(rows.astype(F32))
        return (unit * gain_key).astype(BF16)

    def scores_of(half, rows, side, part, seen):
        weight = jnp.where(seen, jnp.exp2(mm(half, q_t[side, :, part]) * EXP2), 0.0)
        return weight, mm(rows, u_t[side, :, part])

    def visible(step):
        owner = lax.rem(chip + step, chips) * 2 + core
        return lax.broadcasted_iota(jnp.int32, (ROWS, CHUNK), 0) + owner * ROWS < length

    key_place = lax.broadcasted_iota(jnp.int32, (ROWS, CHUNK), 0)
    token = lax.rem(lax.broadcasted_iota(jnp.int32, (ROWS, CHUNK), 1), ROWS)
    first_keys = [half_of(r_in[:, :HEAD]), half_of(kv[0, :, :HEAD])]
    first_values = [r_in[:, HEAD:], kv[0, :, HEAD:]]
    first_seen = [key_place <= token, visible(0)]
    first_weights = [self_weights, weights.at[0, 0]]
    first_marks = [self_marks, marks.at[0, 0]]
    for part in chunks():
        found = [
            scores_of(half, rows, 0, part, seen) for half, rows, seen in zip(first_keys, first_values, first_seen)
        ]
        den = fold(found[0][0]) + fold(found[1][0])
        mean = jnp.sum(fold(found[0][0] * found[0][1]) + fold(found[1][0] * found[1][1]), axis=0, keepdims=True)
        mean = mean / jnp.sum(den, axis=0, keepdims=True)
        base[0, :, part] = jnp.broadcast_to(mean, den.shape)
        den_sum[0, :, part] = den
        mark_total = jnp.zeros_like(den)
        for (weight, probe), weight_ref, mark_ref in zip(found, first_weights, first_marks):
            mark = weight * (probe - mean)
            mark_total += fold(mark)
            weight_ref[:, part] = weight.astype(BF16)
            mark_ref[:, part] = mark.astype(BF16)
        mark_sum[0, :, part] = mark_total
    send_base = twin(2, base.at[0], base.at[1])
    send_base.start()

    send_reward.wait_recv()
    pair = reward_in[chips], reward_in[chips + 1]
    row = lax.broadcasted_iota(jnp.int32, (8, 128), 0)
    reward_in[0] = jnp.where(row == 0, pair[0] + pair[1], pair[0] * pair[0] + pair[1] * pair[1])

    @pl.loop(1, chips)
    def _(step):
        reward_copy(step).start()

    first_t = jnp.transpose(jnp.concatenate(first_keys, axis=0))
    for part in chunks():
        mark_grads[0, :, part] += mm(first_t, jnp.concatenate([ref[:, part] for ref in first_marks], axis=0))
        weight_grads[0, :, part] += mm(first_t, jnp.concatenate([ref[:, part] for ref in first_weights], axis=0))

    def forward(step, sides):
        half = half_of(kv[step, :, :HEAD])
        half_t = jnp.transpose(half)
        seen = visible(step)
        for side in sides:
            for part in chunks():
                weight, probe = scores_of(half, kv[step, :, HEAD:], side, part, seen)
                mark = weight * (probe - base[side, 0:1, part])
                den_sum[side, :, part] += fold(weight)
                mark_sum[side, :, part] += fold(mark)
                weights[step, side, :, part] = weight.astype(BF16)
                marks[step, side, :, part] = mark.astype(BF16)
        for side in sides:
            for part in chunks():
                mark_grads[side, :, part] += mm(half_t, marks[step, side, :, part])
                weight_grads[side, :, part] += mm(half_t, weights[step, side, :, part])

    send_q.wait_recv()
    send_u.wait_recv()
    send_base.wait_recv()
    forward(0, [1])

    @pl.loop(1, chips)
    def _(step):
        gather(chips - step).wait_recv()
        forward(step, [0, 1])

    for side in range(2):
        den = jnp.sum(den_sum[side], axis=0, keepdims=True)
        total = jnp.sum(mark_sum[side], axis=0, keepdims=True)
        place = lax.broadcasted_iota(jnp.int32, (8, QUERIES), 0)
        stat_out[side] = jnp.where(place == 0, den, total)
    send_stat = twin(4, stat_out, stat_in)
    send_stat.start()

    @pl.loop(1, chips)
    def _(step):
        reward_copy(chips - step).wait_recv()

    total = reward_in[0]
    for step in range(1, chips):
        total = total + reward_in[step]
    group = float(responses)
    reward_total, squares = total[0:1, 0:1], total[1:2, 0:1]
    spread = jnp.sqrt(group * squares - reward_total * reward_total) / group
    advantages = [
        (reward_in[chips + side, 0:1, 0:1] - reward_total / group) / jnp.maximum(spread, 1.0) for side in range(2)
    ]

    send_stat.wait_recv()
    inverse_den, delta, value_factor, key_factor = [], [], [], []
    for side in range(2):
        both = stat_out[side] + stat_in[1 - side]
        inverse_den.append(1.0 / both[0:1, :])
        delta.append(both[1:2, :] * inverse_den[side])
        value_factor.append(inverse_den[side] * advantages[side])
        key_factor.append(value_factor[side] * SCALE)

    plane_base = 2
    z_base = plane_base + 2 * chips
    z_own = z_base + planes

    def gain_plane(step):
        back = lax.rem(chips - lax.rem(step, chips), chips) + (step // chips) * chips
        return remote(
            gain_buf.at[plane_base],
            gain_buf.at[plane_base + back],
            gain_send.at[plane_base + step],
            gain_recv.at[plane_base + back],
            to_plane(step),
        )

    def gain_z(step):
        return remote(
            gain_buf.at[z_own],
            gain_buf.at[z_base + planes - step],
            gain_send.at[z_base + step],
            gain_recv.at[z_base + planes - step],
            to_z(step),
        )

    query_total = jnp.zeros((HEAD, ROWS), F32)
    for side in range(2):
        for part in heads():
            grad_t = mark_grads[side, :, part] - weight_grads[side, :, part] * delta[side][:, part]
            grad_t = grad_t * key_factor[side][:, part]
            mark_grads[side, :, part] = grad_t
            query_total += grad_t * q_t[side, :, part].astype(F32)
    shared = jnp.sum(fold(jnp.transpose(query_total)), axis=0, keepdims=True)
    gain_buf[0] = jnp.where(row == 0, shared / gain_query, jnp.where(row == 1, shared / gain_key, 0.0))
    send_gain = twin(6, gain_buf.at[0], gain_buf.at[1])
    send_gain.start()
    send_grad = twin(5, mark_grads.at[1], grad_in)
    send_grad.start()

    for side in range(2):
        for part in heads():
            scaled = q_t[side, :, part].astype(F32) * key_factor[side][:, part]
            raised = u_t[side, :, part].astype(F32) * value_factor[side][:, part]
            key_rows[side, part, :] = jnp.transpose(scaled.astype(BF16))
            value_rows[side, part, :HEAD] = jnp.transpose((scaled * -delta[side][:, part]).astype(BF16))
            value_rows[side, part, HEAD:] = jnp.transpose(raised.astype(BF16))

    def part_copy(step):
        return remote(
            part_out.at[step], part_in.at[chips - step], part_send.at[step], part_recv.at[chips - step], to_chip(step)
        )

    def key_grads(weight, mark, side):
        both = mm(weight, value_rows[side])
        return both[:, :HEAD] + mm(mark, key_rows[side]), both[:, HEAD:]

    def backward(first, count):
        sums = [
            key_grads(
                weights[first : first + count, side].reshape(count * ROWS, QUERIES),
                marks[first : first + count, side].reshape(count * ROWS, QUERIES),
                side,
            )
            for side in range(2)
        ]
        grad_key, grad_value = sums[0][0] + sums[1][0], sums[0][1] + sums[1][1]
        for at in reversed(range(count)):
            rows = slice(at * ROWS, (at + 1) * ROWS)
            if first + at:
                part_out[first + at, :, :HEAD] = grad_key[rows].astype(BF16)
                part_out[first + at, :, HEAD:] = grad_value[rows].astype(BF16)
                part_copy(first + at).start()
        return grad_key[:ROWS], grad_value[:ROWS]

    quarter = chips // 4
    backward(3 * quarter, quarter)
    send_gain.wait_recv()
    gain_buf[plane_base] = gain_buf[0] + gain_buf[1]

    @pl.loop(1, 2 * chips)
    def _(step):
        gain_plane(step).start()

    backward(2 * quarter, quarter)
    sum_key, sum_value = backward(0, 2 * quarter)
    self_key, self_value = key_grads(self_weights[...], self_marks[...], 0)

    unit, inverse = unit_scale(r_in[:, :HEAD].astype(F32))
    response_out[:, :HEAD] = unit_back(self_key, unit, inverse, gain_key)
    response_out[:, HEAD:] = self_value
    send_grad.wait_recv()
    for part in heads():
        grad_normed = jnp.transpose(mark_grads[0, :, part] + grad_in[:, part])
        unit, inverse = unit_scale(q_in[:, part].astype(F32))
        query_out[:, part] = unit_back(grad_normed, unit, inverse, gain_query)
    out_copies = [
        pltpu.make_async_copy(query_out, grad_query, out_sem.at[0]),
        pltpu.make_async_copy(response_out, grad_response, out_sem.at[1]),
        pltpu.make_async_copy(prefix_out, grad_prefix, out_sem.at[2]),
        pltpu.make_async_copy(gain_out, gain_grads, out_sem.at[3]),
    ]
    out_copies[0].start()
    out_copies[1].start()

    @pl.loop(1, 2 * chips)
    def _(step):
        gain_plane(step).wait_recv()

    total = gain_buf[plane_base]
    for step in range(1, 2 * chips):
        total = total + gain_buf[plane_base + step]
    gain_buf[z_own] = total

    @pl.loop(1, planes)
    def _(step):
        gain_z(step).start()

    for step in range(1, chips):
        part_copy(chips - step).wait_recv()
        sum_key += part_in[step, :, :HEAD].astype(F32)
        sum_value += part_in[step, :, HEAD:].astype(F32)
    unit, inverse = unit_scale(kv[0, :, :HEAD].astype(F32))
    prefix_out[:, :HEAD] = unit_back(sum_key, unit, inverse, gain_key)
    prefix_out[:, HEAD:] = sum_value
    out_copies[2].start()

    for copy in (send_q, send_u, send_base, send_reward, send_stat, send_grad, send_gain):
        copy.wait_send()

    @pl.loop(1, chips)
    def _(step):
        gather(step).wait_send()
        reward_copy(step).wait_send()
        part_copy(step).wait_send()

    @pl.loop(1, 2 * chips)
    def _(step):
        gain_plane(step).wait_send()

    @pl.loop(1, planes)
    def _(step):
        gain_z(step).wait_recv()

    total = gain_buf[z_own]
    for step in range(1, planes):
        total = total + gain_buf[z_base + step]
    gain_out[...] = total[0:2, :] / math.sqrt(prompts * responses * ROWS)
    out_copies[3].start()

    @pl.loop(1, planes)
    def _(step):
        gain_z(step).wait_send()

    for copy in out_copies:
        copy.wait()


def hand_on(*refs):
    half = len(refs) // 2
    for taken, given in zip(refs[:half], refs[half:]):
        given[...] = taken[...]


def local(queries, resp_kv, prefix_kv, upstream, gains, rewards, lengths):
    prompts, responses = lax.axis_size("prompt"), lax.axis_size("resp")
    chips, planes = responses // 2, prompts // 2
    gain_slots = 2 + 2 * chips + planes + 1
    hbm = pl.BlockSpec(memory_space=pltpu.HBM)
    vmem = pl.BlockSpec(memory_space=pltpu.VMEM)
    dma = pltpu.SemaphoreType.DMA
    shapes = (
        jax.ShapeDtypeStruct((ROWS, QUERIES), F32),
        jax.ShapeDtypeStruct((ROWS, 2 * HEAD), F32),
        jax.ShapeDtypeStruct((ROWS, 2 * HEAD), F32),
        jax.ShapeDtypeStruct((2, HEAD), F32),
    )
    found = pl.pallas_call(
        functools.partial(kernel, (prompts, responses)),
        out_shape=shapes,
        in_specs=[hbm] * 7,
        out_specs=(hbm,) * 4,
        scratch_shapes=[
            pltpu.VMEM((ROWS, QUERIES), BF16),
            pltpu.VMEM((ROWS, QUERIES), BF16),
            pltpu.VMEM((ROWS, 2 * HEAD), BF16),
            pltpu.VMEM((2, HEAD), F32),
            pltpu.SMEM((1, 1), jnp.int32),
            pltpu.SMEM((1,), jnp.int32),
            pltpu.VMEM((chips, ROWS, 2 * HEAD), BF16),
            pltpu.VMEM((2, HEAD, QUERIES), BF16),
            pltpu.VMEM((2, HEAD, QUERIES), BF16),
            pltpu.VMEM((2, QUERIES, HEAD), BF16),
            pltpu.VMEM((2, QUERIES, 2 * HEAD), BF16),
            pltpu.VMEM((chips, 2, ROWS, QUERIES), BF16),
            pltpu.VMEM((chips, 2, ROWS, QUERIES), BF16),
            pltpu.VMEM((ROWS, QUERIES), BF16),
            pltpu.VMEM((ROWS, QUERIES), BF16),
            pltpu.VMEM((2, 8, QUERIES), F32),
            pltpu.VMEM((2, 8, QUERIES), F32),
            pltpu.VMEM((2, 8, QUERIES), F32),
            pltpu.VMEM((2, HEAD, QUERIES), F32),
            pltpu.VMEM((2, HEAD, QUERIES), F32),
            pltpu.VMEM((2, 8, QUERIES), F32),
            pltpu.VMEM((2, 8, QUERIES), F32),
            pltpu.VMEM((HEAD, QUERIES), F32),
            pltpu.VMEM((chips + 2, 8, 128), F32),
            pltpu.VMEM((chips, ROWS, 2 * HEAD), BF16),
            pltpu.VMEM((chips, ROWS, 2 * HEAD), BF16),
            pltpu.VMEM((gain_slots, 8, HEAD), F32),
            pltpu.VMEM((ROWS, QUERIES), F32),
            pltpu.VMEM((ROWS, 2 * HEAD), F32),
            pltpu.VMEM((ROWS, 2 * HEAD), F32),
            pltpu.VMEM((2, HEAD), F32),
            dma((7,)),
            dma((4,)),
            dma((chips,)),
            dma((chips,)),
            dma((chips,)),
            dma((chips,)),
            dma((chips,)),
            dma((chips,)),
            dma((7,)),
            dma((7,)),
            dma((gain_slots,)),
            dma((gain_slots,)),
        ],
        compiler_params=pltpu.CompilerParams(
            collective_id=0, has_side_effects=True, vmem_limit_bytes=VMEM_LIMIT
        ),
    )(queries, resp_kv, prefix_kv, upstream, gains, rewards, lengths)
    return pl.pallas_call(
        hand_on,
        out_shape=shapes,
        in_specs=[vmem] * 4,
        out_specs=(vmem,) * 4,
        compiler_params=pltpu.CompilerParams(vmem_limit_bytes=VMEM_LIMIT),
    )(*found)


def solution(mesh):
    rows = P(("prompt", "resp"), None)
    return jax.shard_map(
        local,
        mesh=mesh,
        in_specs=(rows, rows, rows, rows, P(), P("prompt", "resp"), P("prompt")),
        out_specs=(rows, rows, rows, P()),
        check_vma=False,
    )
```

```python
import functools
import math

import jax
import jax.numpy as jnp
from jax import lax
from jax.experimental import pallas as pl
from jax.experimental.pallas import tpu as pltpu
from jax.sharding import PartitionSpec as P

HEAD = 128
HEADS = 8
ROWS = 128
QUERIES = HEADS * ROWS
CHUNK = 256
VMEM_LIMIT = 63 * 1024 * 1024
EPS = 1e-06
SCALE = HEAD ** (-0.5)
EXP2 = SCALE * math.log2(math.e)
MESH = pl.DeviceIdType.MESH
F32 = jnp.float32
BF16 = jnp.bfloat16


def unit_scale(values):
    inverse = lax.rsqrt(jnp.mean(values * values, axis=-1, keepdims=True) + EPS)
    return values * inverse, inverse


def unit_back(grad_normed, unit_values, inverse, gain):
    grad_unit = grad_normed * gain
    inner = jnp.mean(grad_unit * unit_values, axis=-1, keepdims=True)
    return inverse * (grad_unit - unit_values * inner)


def fold(values):
    rows, columns = values.shape
    return jnp.sum(values.reshape(rows // 8, 8, columns), axis=0)


def mm(left, right):
    return lax.dot_general(left, right, (((1,), (0,)), ((), ())), preferred_element_type=F32)


def chunks():
    return [slice(start, start + CHUNK) for start in range(0, QUERIES, CHUNK)]


def offset(slot):
    if isinstance(slot, int):
        return slot * 3 % 8 // 2 % 4, 2 * slot * (slot - 1) % 11 % 2
    return lax.rem(lax.div(lax.rem(slot * 3, 8), 2), 4), lax.rem(lax.rem(2 * slot * (slot - 1), 11), 2)


def mirror(slot):
    along, across = offset(slot)
    return next(other for other in range(8) if offset(other) == ((4 - along) % 4, across))


def heads():
    return [slice(h * HEAD, (h + 1) * HEAD) for h in range(HEADS)]


def kernel(
    sizes,
    queries,
    resp_kv,
    prefix_kv,
    upstream,
    gains,
    rewards,
    lengths,
    grad_query,
    grad_response,
    grad_prefix,
    gain_grads,
    q_in,
    u_in,
    r_in,
    g_in,
    reward_word,
    length_word,
    kv,
    q_t,
    u_t,
    key_rows,
    value_rows,
    weights,
    marks,
    self_weights,
    self_marks,
    den_sum,
    mark_sum,
    base,
    mark_grads,
    weight_grads,
    stat_out,
    stat_in,
    grad_in,
    reward_in,
    part_out,
    part_in,
    gain_buf,
    query_out,
    response_out,
    prefix_out,
    gain_out,
    in_sem,
    out_sem,
    ag_send,
    ag_recv,
    reward_send,
    reward_recv,
    part_send,
    part_recv,
    twin_send,
    twin_recv,
    gain_send,
    gain_recv,
):
    prompts, responses = sizes
    chips = responses // 2
    planes = prompts // 2
    prompt = lax.axis_index("prompt")
    resp = lax.axis_index("resp")
    chip = resp // 2
    core = lax.rem(resp, 2)
    low = lax.rem(prompt, 2)

    def place_of(slot):
        along, across = offset(slot)
        return lax.rem(lax.div(chip, 2) + along, chips // 2) * 2 + lax.rem(chip + across, 2)

    def to_chip(slot):
        return (prompt, place_of(slot) * 2 + core)

    sibling = (prompt, resp + 1 - 2 * core)

    def to_plane(step):
        row = lax.rem(low + step // chips, 2)
        return (prompt - low + row, lax.rem(chip + lax.rem(step, chips), chips) * 2 + core)

    def to_z(step):
        return (lax.rem(prompt + 2 * step, prompts), resp)

    barrier = pltpu.get_barrier_semaphore()

    def greet(device):
        pl.semaphore_signal(barrier, inc=1, device_id=device, device_id_type=MESH)

    copies = [
        pltpu.make_async_copy(prefix_kv, kv.at[0], in_sem.at[0]),
        pltpu.make_async_copy(queries, q_in, in_sem.at[1]),
        pltpu.make_async_copy(upstream, u_in, in_sem.at[2]),
        pltpu.make_async_copy(resp_kv, r_in, in_sem.at[3]),
        pltpu.make_async_copy(gains, g_in, in_sem.at[4]),
        pltpu.make_async_copy(rewards, reward_word, in_sem.at[5]),
        pltpu.make_async_copy(lengths, length_word, in_sem.at[6]),
    ]
    for copy in copies:
        copy.start()

    @pl.loop(1, planes)
    def _(step):
        greet(to_z(step))

    @pl.loop(1, 2 * chips)
    def _(step):
        greet(to_plane(step))

    greet(sibling)

    copies[0].wait()
    pl.semaphore_wait(barrier, 1 + (2 * chips - 1) + (planes - 1))

    def remote(src, dst, send, recv, device):
        return pltpu.make_async_remote_copy(
            src_ref=src, dst_ref=dst, send_sem=send, recv_sem=recv, device_id=device, device_id_type=MESH
        )

    def gather(slot):
        return remote(kv.at[0], kv.at[mirror(slot)], ag_send.at[slot], ag_recv.at[mirror(slot)], to_chip(slot))

    def arrival(slot):
        return remote(kv.at[0], kv.at[slot], ag_send.at[slot], ag_recv.at[slot], sibling)

    def twin(place, src, dst):
        return remote(src, dst, twin_send.at[place], twin_recv.at[place], sibling)

    def reward_copy(slot):
        return remote(
            reward_in.at[0],
            reward_in.at[mirror(slot)],
            reward_send.at[slot],
            reward_recv.at[mirror(slot)],
            to_chip(slot),
        )

    for slot in (1, 2, 3):
        gather(slot).start()
    for copy in copies[1:]:
        copy.wait()
    own_reward = reward_word[0, 0].astype(F32)
    reward_in[chips] = jnp.full((8, 128), own_reward, F32)
    send_reward = twin(3, reward_in.at[chips], reward_in.at[chips + 1])
    send_reward.start()

    gain_query = g_in[0:1, :]
    gain_key = g_in[1:2, :]
    length = length_word[0]

    row = lax.broadcasted_iota(jnp.int32, (8, 128), 0)
    for h, part in enumerate(heads()):
        for slot in {0: (4,), 2: (5, 6), 4: (7,)}.get(h, ()):
            gather(slot).start()
        if h == 4:
            send_reward.wait_recv()
            pair = reward_in[chips], reward_in[chips + 1]
            reward_in[0] = jnp.where(row == 0, pair[0] + pair[1], pair[0] * pair[0] + pair[1] * pair[1])
            for slot in range(1, chips):
                reward_copy(slot).start()
        unit, _ = unit_scale(q_in[:, part].astype(F32))
        q_t[0, :, part] = jnp.transpose((unit * gain_query).astype(BF16))
        u_t[0, :, part] = jnp.transpose(u_in[:, part])
    send_q = twin(0, q_t.at[0], q_t.at[1])
    send_u = twin(1, u_t.at[0], u_t.at[1])
    send_q.start()
    send_u.start()
    mark_grads[...] = jnp.zeros_like(mark_grads)
    weight_grads[...] = jnp.zeros_like(weight_grads)
    den_sum[1] = jnp.zeros_like(den_sum[1])
    mark_sum[1] = jnp.zeros_like(mark_sum[1])

    def half_of(rows):
        unit, _ = unit_scale(rows.astype(F32))
        return (unit * gain_key).astype(BF16)

    def scores_of(half, rows, side, part, seen):
        weight = jnp.where(seen, jnp.exp2(mm(half, q_t[side, :, part]) * EXP2), 0.0)
        return weight, mm(rows, u_t[side, :, part])

    def visible(step):
        owner = place_of(step) * 2 + core
        return lax.broadcasted_iota(jnp.int32, (ROWS, CHUNK), 0) + owner * ROWS < length

    key_place = lax.broadcasted_iota(jnp.int32, (ROWS, CHUNK), 0)
    token = lax.rem(lax.broadcasted_iota(jnp.int32, (ROWS, CHUNK), 1), ROWS)
    first_keys = [half_of(r_in[:, :HEAD]), half_of(kv[0, :, :HEAD])]
    first_values = [r_in[:, HEAD:], kv[0, :, HEAD:]]
    first_seen = [key_place <= token, visible(0)]
    first_weights = [self_weights, weights.at[0, 0]]
    first_marks = [self_marks, marks.at[0, 0]]
    for part in chunks():
        found = [
            scores_of(half, rows, 0, part, seen) for half, rows, seen in zip(first_keys, first_values, first_seen)
        ]
        den = fold(found[0][0]) + fold(found[1][0])
        mean = jnp.sum(fold(found[0][0] * found[0][1]) + fold(found[1][0] * found[1][1]), axis=0, keepdims=True)
        mean = mean / jnp.sum(den, axis=0, keepdims=True)
        base[0, :, part] = jnp.broadcast_to(mean, den.shape)
        den_sum[0, :, part] = den
        mark_total = jnp.zeros_like(den)
        for (weight, probe), weight_ref, mark_ref in zip(found, first_weights, first_marks):
            mark = weight * (probe - mean)
            mark_total += fold(mark)
            weight_ref[:, part] = weight.astype(BF16)
            mark_ref[:, part] = mark.astype(BF16)
        mark_sum[0, :, part] = mark_total
    send_base = twin(2, base.at[0], base.at[1])
    send_base.start()

    first_t = jnp.transpose(jnp.concatenate(first_keys, axis=0))
    for part in chunks():
        mark_grads[0, :, part] += mm(first_t, jnp.concatenate([ref[:, part] for ref in first_marks], axis=0))
        weight_grads[0, :, part] += mm(first_t, jnp.concatenate([ref[:, part] for ref in first_weights], axis=0))

    def forward(step, sides):
        half = half_of(kv[step, :, :HEAD])
        half_t = jnp.transpose(half)
        seen = visible(step)
        for side in sides:
            for part in chunks():
                weight, probe = scores_of(half, kv[step, :, HEAD:], side, part, seen)
                mark = weight * (probe - base[side, 0:1, part])
                den_sum[side, :, part] += fold(weight)
                mark_sum[side, :, part] += fold(mark)
                weights[step, side, :, part] = weight.astype(BF16)
                marks[step, side, :, part] = mark.astype(BF16)
        for side in sides:
            for part in chunks():
                mark_grads[side, :, part] += mm(half_t, marks[step, side, :, part])
                weight_grads[side, :, part] += mm(half_t, weights[step, side, :, part])

    send_q.wait_recv()
    send_u.wait_recv()
    send_base.wait_recv()
    forward(0, [1])

    @pl.loop(1, chips)
    def _(step):
        arrival(step).wait_recv()
        forward(step, [0, 1])

    for side in range(2):
        den = jnp.sum(den_sum[side], axis=0, keepdims=True)
        total = jnp.sum(mark_sum[side], axis=0, keepdims=True)
        place = lax.broadcasted_iota(jnp.int32, (8, QUERIES), 0)
        stat_out[side] = jnp.where(place == 0, den, total)
    send_stat = twin(4, stat_out, stat_in)
    send_stat.start()

    total = reward_in[0]
    for step in range(1, chips):
        reward_copy(mirror(step)).wait_recv()
        total = total + reward_in[step]
    group = float(responses)
    reward_total, squares = total[0:1, 0:1], total[1:2, 0:1]
    spread = jnp.sqrt(group * squares - reward_total * reward_total) / group
    advantages = [
        (reward_in[chips + side, 0:1, 0:1] - reward_total / group) / jnp.maximum(spread, 1.0) for side in range(2)
    ]

    send_stat.wait_recv()
    inverse_den, delta, value_factor, key_factor = [], [], [], []
    for side in range(2):
        both = stat_out[side] + stat_in[1 - side]
        inverse_den.append(1.0 / both[0:1, :])
        delta.append(both[1:2, :] * inverse_den[side])
        value_factor.append(inverse_den[side] * advantages[side])
        key_factor.append(value_factor[side] * SCALE)

    plane_base = 2
    z_base = plane_base + 2 * chips
    z_own = z_base + planes

    def gain_plane(step):
        back = lax.rem(chips - lax.rem(step, chips), chips) + (step // chips) * chips
        return remote(
            gain_buf.at[plane_base],
            gain_buf.at[plane_base + back],
            gain_send.at[plane_base + step],
            gain_recv.at[plane_base + back],
            to_plane(step),
        )

    def gain_z(step):
        return remote(
            gain_buf.at[z_own],
            gain_buf.at[z_base + planes - step],
            gain_send.at[z_base + step],
            gain_recv.at[z_base + planes - step],
            to_z(step),
        )

    query_total = jnp.zeros((HEAD, ROWS), F32)
    for side in range(2):
        for part in heads():
            grad_t = mark_grads[side, :, part] - weight_grads[side, :, part] * delta[side][:, part]
            grad_t = grad_t * key_factor[side][:, part]
            mark_grads[side, :, part] = grad_t
            query_total += grad_t * q_t[side, :, part].astype(F32)
    shared = jnp.sum(fold(jnp.transpose(query_total)), axis=0, keepdims=True)
    gain_buf[0] = jnp.where(row == 0, shared / gain_query, jnp.where(row == 1, shared / gain_key, 0.0))
    send_gain = twin(6, gain_buf.at[0], gain_buf.at[1])
    send_gain.start()
    send_grad = twin(5, mark_grads.at[1], grad_in)
    send_grad.start()

    for side in range(2):
        for part in heads():
            scaled = q_t[side, :, part].astype(F32) * key_factor[side][:, part]
            raised = u_t[side, :, part].astype(F32) * value_factor[side][:, part]
            key_rows[side, part, :] = jnp.transpose(scaled.astype(BF16))
            value_rows[side, part, :HEAD] = jnp.transpose((scaled * -delta[side][:, part]).astype(BF16))
            value_rows[side, part, HEAD:] = jnp.transpose(raised.astype(BF16))

    def part_copy(step):
        return remote(
            part_out.at[step], part_in.at[mirror(step)], part_send.at[step], part_recv.at[mirror(step)], to_chip(step)
        )

    def key_grads(weight, mark, side):
        both = mm(weight, value_rows[side])
        return both[:, :HEAD] + mm(mark, key_rows[side]), both[:, HEAD:]

    def backward(first, count):
        sums = [
            key_grads(
                weights[first : first + count, side].reshape(count * ROWS, QUERIES),
                marks[first : first + count, side].reshape(count * ROWS, QUERIES),
                side,
            )
            for side in range(2)
        ]
        grad_key, grad_value = sums[0][0] + sums[1][0], sums[0][1] + sums[1][1]
        for at in reversed(range(count)):
            rows = slice(at * ROWS, (at + 1) * ROWS)
            if first + at:
                part_out[first + at, :, :HEAD] = grad_key[rows].astype(BF16)
                part_out[first + at, :, HEAD:] = grad_value[rows].astype(BF16)
                part_copy(first + at).start()
        return grad_key[:ROWS], grad_value[:ROWS]

    quarter = chips // 4
    send_gain.wait_recv()
    gain_buf[z_own] = gain_buf[0] + gain_buf[1]

    @pl.loop(1, planes)
    def _(step):
        gain_z(step).start()

    backward(3 * quarter, quarter)
    backward(2 * quarter, quarter)
    sum_key, sum_value = backward(0, 2 * quarter)
    self_key, self_value = key_grads(self_weights[...], self_marks[...], 0)

    unit, inverse = unit_scale(r_in[:, :HEAD].astype(F32))
    response_out[:, :HEAD] = unit_back(self_key, unit, inverse, gain_key)
    response_out[:, HEAD:] = self_value
    send_grad.wait_recv()
    for part in heads():
        grad_normed = jnp.transpose(mark_grads[0, :, part] + grad_in[:, part])
        unit, inverse = unit_scale(q_in[:, part].astype(F32))
        query_out[:, part] = unit_back(grad_normed, unit, inverse, gain_query)
    out_copies = [
        pltpu.make_async_copy(query_out, grad_query, out_sem.at[0]),
        pltpu.make_async_copy(response_out, grad_response, out_sem.at[1]),
        pltpu.make_async_copy(prefix_out, grad_prefix, out_sem.at[2]),
        pltpu.make_async_copy(gain_out, gain_grads, out_sem.at[3]),
    ]
    out_copies[0].start()
    out_copies[1].start()

    @pl.loop(1, planes)
    def _(step):
        gain_z(step).wait_recv()

    total = gain_buf[z_own]
    for step in range(1, planes):
        total = total + gain_buf[z_base + step]
    gain_buf[plane_base] = total

    @pl.loop(1, 2 * chips)
    def _(step):
        gain_plane(step).start()

    for step in range(1, chips):
        part_copy(mirror(step)).wait_recv()
        sum_key += part_in[step, :, :HEAD].astype(F32)
        sum_value += part_in[step, :, HEAD:].astype(F32)
    unit, inverse = unit_scale(kv[0, :, :HEAD].astype(F32))
    prefix_out[:, :HEAD] = unit_back(sum_key, unit, inverse, gain_key)
    prefix_out[:, HEAD:] = sum_value
    out_copies[2].start()

    for copy in (send_q, send_u, send_base, send_reward, send_stat, send_grad, send_gain):
        copy.wait_send()

    for step in range(1, chips):
        gather(step).wait_send()
        reward_copy(step).wait_send()
        part_copy(step).wait_send()

    @pl.loop(1, planes)
    def _(step):
        gain_z(step).wait_send()

    @pl.loop(1, 2 * chips)
    def _(step):
        gain_plane(step).wait_recv()

    total = gain_buf[plane_base]
    for step in range(1, 2 * chips):
        total = total + gain_buf[plane_base + step]
    gain_out[...] = total[0:2, :] / math.sqrt(prompts * responses * ROWS)
    out_copies[3].start()

    @pl.loop(1, 2 * chips)
    def _(step):
        gain_plane(step).wait_send()

    for copy in out_copies:
        copy.wait()


def hand_on(*refs):
    half = len(refs) // 2
    for taken, given in zip(refs[:half], refs[half:]):
        given[...] = taken[...]


def local(queries, resp_kv, prefix_kv, upstream, gains, rewards, lengths):
    prompts, responses = lax.axis_size("prompt"), lax.axis_size("resp")
    chips, planes = responses // 2, prompts // 2
    gain_slots = 2 + 2 * chips + planes + 1
    hbm = pl.BlockSpec(memory_space=pltpu.HBM)
    vmem = pl.BlockSpec(memory_space=pltpu.VMEM)
    dma = pltpu.SemaphoreType.DMA
    shapes = (
        jax.ShapeDtypeStruct((ROWS, QUERIES), F32),
        jax.ShapeDtypeStruct((ROWS, 2 * HEAD), F32),
        jax.ShapeDtypeStruct((ROWS, 2 * HEAD), F32),
        jax.ShapeDtypeStruct((2, HEAD), F32),
    )
    found = pl.pallas_call(
        functools.partial(kernel, (prompts, responses)),
        out_shape=shapes,
        in_specs=[hbm] * 7,
        out_specs=(hbm,) * 4,
        scratch_shapes=[
            pltpu.VMEM((ROWS, QUERIES), BF16),
            pltpu.VMEM((ROWS, QUERIES), BF16),
            pltpu.VMEM((ROWS, 2 * HEAD), BF16),
            pltpu.VMEM((2, HEAD), F32),
            pltpu.SMEM((1, 1), jnp.int32),
            pltpu.SMEM((1,), jnp.int32),
            pltpu.VMEM((chips, ROWS, 2 * HEAD), BF16),
            pltpu.VMEM((2, HEAD, QUERIES), BF16),
            pltpu.VMEM((2, HEAD, QUERIES), BF16),
            pltpu.VMEM((2, QUERIES, HEAD), BF16),
            pltpu.VMEM((2, QUERIES, 2 * HEAD), BF16),
            pltpu.VMEM((chips, 2, ROWS, QUERIES), BF16),
            pltpu.VMEM((chips, 2, ROWS, QUERIES), BF16),
            pltpu.VMEM((ROWS, QUERIES), BF16),
            pltpu.VMEM((ROWS, QUERIES), BF16),
            pltpu.VMEM((2, 8, QUERIES), F32),
            pltpu.VMEM((2, 8, QUERIES), F32),
            pltpu.VMEM((2, 8, QUERIES), F32),
            pltpu.VMEM((2, HEAD, QUERIES), F32),
            pltpu.VMEM((2, HEAD, QUERIES), F32),
            pltpu.VMEM((2, 8, QUERIES), F32),
            pltpu.VMEM((2, 8, QUERIES), F32),
            pltpu.VMEM((HEAD, QUERIES), F32),
            pltpu.VMEM((chips + 2, 8, 128), F32),
            pltpu.VMEM((chips, ROWS, 2 * HEAD), BF16),
            pltpu.VMEM((chips, ROWS, 2 * HEAD), BF16),
            pltpu.VMEM((gain_slots, 8, HEAD), F32),
            pltpu.VMEM((ROWS, QUERIES), F32),
            pltpu.VMEM((ROWS, 2 * HEAD), F32),
            pltpu.VMEM((ROWS, 2 * HEAD), F32),
            pltpu.VMEM((2, HEAD), F32),
            dma((7,)),
            dma((4,)),
            dma((chips,)),
            dma((chips,)),
            dma((chips,)),
            dma((chips,)),
            dma((chips,)),
            dma((chips,)),
            dma((7,)),
            dma((7,)),
            dma((gain_slots,)),
            dma((gain_slots,)),
        ],
        compiler_params=pltpu.CompilerParams(
            collective_id=0, has_side_effects=True, vmem_limit_bytes=VMEM_LIMIT
        ),
    )(queries, resp_kv, prefix_kv, upstream, gains, rewards, lengths)
    return pl.pallas_call(
        hand_on,
        out_shape=shapes,
        in_specs=[vmem] * 4,
        out_specs=(vmem,) * 4,
        compiler_params=pltpu.CompilerParams(vmem_limit_bytes=VMEM_LIMIT),
    )(*found)


def solution(mesh):
    rows = P(("prompt", "resp"), None)
    return jax.shard_map(
        local,
        mesh=mesh,
        in_specs=(rows, rows, rows, rows, P(), P("prompt", "resp"), P("prompt")),
        out_specs=(rows, rows, rows, P()),
        check_vma=False,
    )
```

```python
import functools
import math

import jax
import jax.numpy as jnp
from jax import lax
from jax.experimental import pallas as pl
from jax.experimental.pallas import tpu as pltpu
from jax.sharding import PartitionSpec as P

HEAD = 128
HEADS = 8
ROWS = 128
QUERIES = HEADS * ROWS
CHUNK = 256
VMEM_LIMIT = 40 * 1024 * 1024
EPS = 1e-06
SCALE = HEAD ** (-0.5)
EXP2 = SCALE * math.log2(math.e)
MESH = pl.DeviceIdType.MESH
F32 = jnp.float32
BF16 = jnp.bfloat16


def unit_scale(values):
    inverse = lax.rsqrt(jnp.mean(values * values, axis=-1, keepdims=True) + EPS)
    return values * inverse, inverse


def unit_back(grad_normed, unit_values, inverse, gain):
    grad_unit = grad_normed * gain
    inner = jnp.mean(grad_unit * unit_values, axis=-1, keepdims=True)
    return inverse * (grad_unit - unit_values * inner)


def fold(values):
    rows, columns = values.shape
    return jnp.sum(values.reshape(rows // 8, 8, columns), axis=0)


def mm(left, right):
    return lax.dot_general(left, right, (((1,), (0,)), ((), ())), preferred_element_type=F32)


def chunks():
    return [slice(start, start + CHUNK) for start in range(0, QUERIES, CHUNK)]


def offset(slot):
    if isinstance(slot, int):
        return slot * 3 % 8 // 2 % 4, 2 * slot * (slot - 1) % 11 % 2
    return lax.rem(lax.div(lax.rem(slot * 3, 8), 2), 4), lax.rem(lax.rem(2 * slot * (slot - 1), 11), 2)


def mirror(slot):
    along, across = offset(slot)
    return next(other for other in range(8) if offset(other) == ((4 - along) % 4, across))


def heads():
    return [slice(h * HEAD, (h + 1) * HEAD) for h in range(HEADS)]


def kernel(
    sizes,
    queries,
    resp_kv,
    prefix_kv,
    upstream,
    gains,
    rewards,
    lengths,
    grad_query,
    grad_response,
    grad_prefix,
    gain_grads,
    q_in,
    u_in,
    r_in,
    g_in,
    kv,
    q_t,
    u_t,
    key_rows,
    value_rows,
    weights,
    marks,
    self_weights,
    self_marks,
    den_sum,
    mark_sum,
    base,
    mark_grads,
    weight_grads,
    stat_out,
    stat_in,
    grad_in,
    reward_in,
    part_out,
    part_in,
    gain_buf,
    in_sem,
    ag_send,
    ag_recv,
    reward_send,
    reward_recv,
    part_send,
    part_recv,
    twin_send,
    twin_recv,
    gain_send,
    gain_recv,
):
    prompts, responses = sizes
    chips = responses // 2
    planes = prompts // 2
    prompt = lax.axis_index("prompt")
    resp = lax.axis_index("resp")
    chip = resp // 2
    core = lax.rem(resp, 2)
    low = lax.rem(prompt, 2)

    def place_of(slot):
        along, across = offset(slot)
        return lax.rem(lax.div(chip, 2) + along, chips // 2) * 2 + lax.rem(chip + across, 2)

    def to_chip(slot):
        return (prompt, place_of(slot) * 2 + core)

    sibling = (prompt, resp + 1 - 2 * core)

    def to_plane(step):
        row = lax.rem(low + step // chips, 2)
        return (prompt - low + row, lax.rem(chip + lax.rem(step, chips), chips) * 2 + core)

    def to_z(step):
        return (lax.rem(prompt + 2 * step, prompts), resp)

    barrier = pltpu.get_barrier_semaphore()

    def greet(device):
        pl.semaphore_signal(barrier, inc=1, device_id=device, device_id_type=MESH)

    copies = [
        pltpu.make_async_copy(prefix_kv, kv.at[0], in_sem.at[0]),
        pltpu.make_async_copy(queries, q_in, in_sem.at[1]),
        pltpu.make_async_copy(upstream, u_in, in_sem.at[2]),
        pltpu.make_async_copy(resp_kv, r_in, in_sem.at[3]),
        pltpu.make_async_copy(gains, g_in, in_sem.at[4]),
    ]
    for copy in copies:
        copy.start()

    @pl.loop(1, planes)
    def _(step):
        greet(to_z(step))

    @pl.loop(1, 2 * chips)
    def _(step):
        greet(to_plane(step))

    greet(sibling)

    copies[0].wait()
    pl.semaphore_wait(barrier, 1 + (2 * chips - 1) + (planes - 1))

    def remote(src, dst, send, recv, device):
        return pltpu.make_async_remote_copy(
            src_ref=src, dst_ref=dst, send_sem=send, recv_sem=recv, device_id=device, device_id_type=MESH
        )

    def gather(slot):
        return remote(kv.at[0], kv.at[mirror(slot)], ag_send.at[slot], ag_recv.at[mirror(slot)], to_chip(slot))

    def arrival(slot):
        return remote(kv.at[0], kv.at[slot], ag_send.at[slot], ag_recv.at[slot], sibling)

    def twin(place, src, dst):
        return remote(src, dst, twin_send.at[place], twin_recv.at[place], sibling)

    def reward_copy(slot):
        return remote(
            reward_in.at[0],
            reward_in.at[mirror(slot)],
            reward_send.at[slot],
            reward_recv.at[mirror(slot)],
            to_chip(slot),
        )

    for slot in (1, 2, 3):
        gather(slot).start()
    for copy in copies[1:]:
        copy.wait()
    own_reward = rewards[0, 0].astype(F32)
    reward_in[chips] = jnp.full((8, 128), own_reward, F32)
    send_reward = twin(3, reward_in.at[chips], reward_in.at[chips + 1])
    send_reward.start()

    gain_query = g_in[0:1, :]
    gain_key = g_in[1:2, :]
    length = lengths[0]

    row = lax.broadcasted_iota(jnp.int32, (8, 128), 0)
    for h, part in enumerate(heads()):
        for slot in {0: (4,), 2: (5, 6), 4: (7,)}.get(h, ()):
            gather(slot).start()
        if h == 4:
            send_reward.wait_recv()
            pair = reward_in[chips], reward_in[chips + 1]
            reward_in[0] = jnp.where(row == 0, pair[0] + pair[1], pair[0] * pair[0] + pair[1] * pair[1])
            for slot in range(1, chips):
                reward_copy(slot).start()
        unit, _ = unit_scale(q_in[:, part].astype(F32))
        q_t[0, :, part] = jnp.transpose((unit * gain_query).astype(BF16))
        u_t[0, :, part] = jnp.transpose(u_in[:, part])
    send_q = twin(0, q_t.at[0], q_t.at[1])
    send_u = twin(1, u_t.at[0], u_t.at[1])
    send_q.start()
    send_u.start()
    mark_grads[...] = jnp.zeros_like(mark_grads)
    weight_grads[...] = jnp.zeros_like(weight_grads)
    den_sum[1] = jnp.zeros_like(den_sum[1])
    mark_sum[1] = jnp.zeros_like(mark_sum[1])

    def half_of(rows):
        unit, _ = unit_scale(rows.astype(F32))
        return (unit * gain_key).astype(BF16)

    def scores_of(half, rows, side, part, seen):
        weight = jnp.where(seen, jnp.exp2(mm(half, q_t[side, :, part]) * EXP2), 0.0)
        return weight, mm(rows, u_t[side, :, part])

    def visible(step):
        owner = place_of(step) * 2 + core
        return lax.broadcasted_iota(jnp.int32, (ROWS, CHUNK), 0) + owner * ROWS < length

    key_place = lax.broadcasted_iota(jnp.int32, (ROWS, CHUNK), 0)
    token = lax.rem(lax.broadcasted_iota(jnp.int32, (ROWS, CHUNK), 1), ROWS)
    first_keys = [half_of(r_in[:, :HEAD]), half_of(kv[0, :, :HEAD])]
    first_values = [r_in[:, HEAD:], kv[0, :, HEAD:]]
    first_seen = [key_place <= token, visible(0)]
    first_weights = [self_weights, weights.at[0, 0]]
    first_marks = [self_marks, marks.at[0, 0]]
    for part in chunks():
        found = [
            scores_of(half, rows, 0, part, seen) for half, rows, seen in zip(first_keys, first_values, first_seen)
        ]
        den = fold(found[0][0]) + fold(found[1][0])
        mean = jnp.sum(fold(found[0][0] * found[0][1]) + fold(found[1][0] * found[1][1]), axis=0, keepdims=True)
        mean = mean / jnp.sum(den, axis=0, keepdims=True)
        base[0, :, part] = jnp.broadcast_to(mean, den.shape)
        den_sum[0, :, part] = den
        mark_total = jnp.zeros_like(den)
        for (weight, probe), weight_ref, mark_ref in zip(found, first_weights, first_marks):
            mark = weight * (probe - mean)
            mark_total += fold(mark)
            weight_ref[:, part] = weight.astype(BF16)
            mark_ref[:, part] = mark.astype(BF16)
        mark_sum[0, :, part] = mark_total
    send_base = twin(2, base.at[0], base.at[1])
    send_base.start()

    first_t = jnp.transpose(jnp.concatenate(first_keys, axis=0))
    for part in chunks():
        mark_grads[0, :, part] += mm(first_t, jnp.concatenate([ref[:, part] for ref in first_marks], axis=0))
        weight_grads[0, :, part] += mm(first_t, jnp.concatenate([ref[:, part] for ref in first_weights], axis=0))

    def forward(step, sides):
        half = half_of(kv[step, :, :HEAD])
        half_t = jnp.transpose(half)
        seen = visible(step)
        for side in sides:
            for part in chunks():
                weight, probe = scores_of(half, kv[step, :, HEAD:], side, part, seen)
                mark = weight * (probe - base[side, 0:1, part])
                den_sum[side, :, part] += fold(weight)
                mark_sum[side, :, part] += fold(mark)
                weights[step, side, :, part] = weight.astype(BF16)
                marks[step, side, :, part] = mark.astype(BF16)
        for side in sides:
            for part in chunks():
                mark_grads[side, :, part] += mm(half_t, marks[step, side, :, part])
                weight_grads[side, :, part] += mm(half_t, weights[step, side, :, part])

    send_q.wait_recv()
    send_u.wait_recv()
    send_base.wait_recv()
    forward(0, [1])

    @pl.loop(1, chips)
    def _(step):
        arrival(step).wait_recv()
        forward(step, [0, 1])

    for side in range(2):
        den = jnp.sum(den_sum[side], axis=0, keepdims=True)
        total = jnp.sum(mark_sum[side], axis=0, keepdims=True)
        place = lax.broadcasted_iota(jnp.int32, (8, QUERIES), 0)
        stat_out[side] = jnp.where(place == 0, den, total)
    send_stat = twin(4, stat_out, stat_in)
    send_stat.start()

    total = reward_in[0]
    for step in range(1, chips):
        reward_copy(mirror(step)).wait_recv()
        total = total + reward_in[step]
    group = float(responses)
    reward_total, squares = total[0:1, 0:1], total[1:2, 0:1]
    spread = jnp.sqrt(group * squares - reward_total * reward_total) / group
    advantages = [
        (reward_in[chips + side, 0:1, 0:1] - reward_total / group) / jnp.maximum(spread, 1.0) for side in range(2)
    ]

    send_stat.wait_recv()
    inverse_den, delta, value_factor, key_factor = [], [], [], []
    for side in range(2):
        both = stat_out[side] + stat_in[1 - side]
        inverse_den.append(1.0 / both[0:1, :])
        delta.append(both[1:2, :] * inverse_den[side])
        value_factor.append(inverse_den[side] * advantages[side])
        key_factor.append(value_factor[side] * SCALE)

    plane_base = 2
    z_base = plane_base + 2 * chips
    z_own = z_base + planes

    def gain_plane(step):
        back = lax.rem(chips - lax.rem(step, chips), chips) + (step // chips) * chips
        return remote(
            gain_buf.at[plane_base],
            gain_buf.at[plane_base + back],
            gain_send.at[plane_base + step],
            gain_recv.at[plane_base + back],
            to_plane(step),
        )

    def gain_z(step):
        return remote(
            gain_buf.at[z_own],
            gain_buf.at[z_base + planes - step],
            gain_send.at[z_base + step],
            gain_recv.at[z_base + planes - step],
            to_z(step),
        )

    query_total = jnp.zeros((HEAD, ROWS), F32)
    for side in range(2):
        for part in heads():
            grad_t = mark_grads[side, :, part] - weight_grads[side, :, part] * delta[side][:, part]
            grad_t = grad_t * key_factor[side][:, part]
            mark_grads[side, :, part] = grad_t
            query_total += grad_t * q_t[side, :, part].astype(F32)
    shared = jnp.sum(fold(jnp.transpose(query_total)), axis=0, keepdims=True)
    gain_buf[z_own] = jnp.where(row == 0, shared / gain_query, jnp.where(row == 1, shared / gain_key, 0.0))

    @pl.loop(1, planes)
    def _(step):
        gain_z(step).start()

    send_grad = twin(5, mark_grads.at[1], grad_in)
    send_grad.start()

    for side in range(2):
        for part in heads():
            scaled = q_t[side, :, part].astype(F32) * key_factor[side][:, part]
            raised = u_t[side, :, part].astype(F32) * value_factor[side][:, part]
            key_rows[side, part, :] = jnp.transpose(scaled.astype(BF16))
            value_rows[side, part, :HEAD] = jnp.transpose((scaled * -delta[side][:, part]).astype(BF16))
            value_rows[side, part, HEAD:] = jnp.transpose(raised.astype(BF16))

    def part_copy(step):
        return remote(
            part_out.at[step], part_in.at[mirror(step)], part_send.at[step], part_recv.at[mirror(step)], to_chip(step)
        )

    def key_grads(weight, mark, side):
        both = mm(weight, value_rows[side])
        return both[:, :HEAD] + mm(mark, key_rows[side]), both[:, HEAD:]

    def backward(first, count):
        sums = [
            key_grads(
                weights[first : first + count, side].reshape(count * ROWS, QUERIES),
                marks[first : first + count, side].reshape(count * ROWS, QUERIES),
                side,
            )
            for side in range(2)
        ]
        grad_key, grad_value = sums[0][0] + sums[1][0], sums[0][1] + sums[1][1]
        for at in reversed(range(count)):
            rows = slice(at * ROWS, (at + 1) * ROWS)
            if first + at:
                part_out[first + at, :, :HEAD] = grad_key[rows].astype(BF16)
                part_out[first + at, :, HEAD:] = grad_value[rows].astype(BF16)
                part_copy(first + at).start()
        return grad_key[:ROWS], grad_value[:ROWS]

    quarter = chips // 4
    backward(3 * quarter, quarter)
    backward(2 * quarter, quarter)
    sum_key, sum_value = backward(0, 2 * quarter)
    self_key, self_value = key_grads(self_weights[...], self_marks[...], 0)

    unit, inverse = unit_scale(r_in[:, :HEAD].astype(F32))
    grad_response[:, :HEAD] = unit_back(self_key, unit, inverse, gain_key)
    grad_response[:, HEAD:] = self_value
    send_grad.wait_recv()
    for part in heads():
        grad_normed = jnp.transpose(mark_grads[0, :, part] + grad_in[:, part])
        unit, inverse = unit_scale(q_in[:, part].astype(F32))
        grad_query[:, part] = unit_back(grad_normed, unit, inverse, gain_query)
    @pl.loop(1, planes)
    def _(step):
        gain_z(step).wait_recv()

    total = gain_buf[z_own]
    for step in range(1, planes):
        total = total + gain_buf[z_base + step]
    gain_buf[0] = total
    send_gain = twin(6, gain_buf.at[0], gain_buf.at[1])
    send_gain.start()
    send_gain.wait_recv()
    gain_buf[plane_base] = gain_buf[0] + gain_buf[1]

    @pl.loop(1, 2 * chips)
    def _(step):
        gain_plane(step).start()

    for step in range(1, chips):
        part_copy(mirror(step)).wait_recv()
        sum_key += part_in[step, :, :HEAD].astype(F32)
        sum_value += part_in[step, :, HEAD:].astype(F32)
    unit, inverse = unit_scale(kv[0, :, :HEAD].astype(F32))
    grad_prefix[:, :HEAD] = unit_back(sum_key, unit, inverse, gain_key)
    grad_prefix[:, HEAD:] = sum_value

    for copy in (send_q, send_u, send_base, send_reward, send_stat, send_grad, send_gain):
        copy.wait_send()

    for step in range(1, chips):
        gather(step).wait_send()
        reward_copy(step).wait_send()
        part_copy(step).wait_send()

    @pl.loop(1, planes)
    def _(step):
        gain_z(step).wait_send()

    @pl.loop(1, 2 * chips)
    def _(step):
        gain_plane(step).wait_recv()

    total = gain_buf[plane_base]
    for step in range(1, 2 * chips):
        total = total + gain_buf[plane_base + step]
    gain_grads[...] = total[0:2, :] / math.sqrt(prompts * responses * ROWS)

    @pl.loop(1, 2 * chips)
    def _(step):
        gain_plane(step).wait_send()


def hand_on(*refs):
    half = len(refs) // 2
    for taken, given in zip(refs[:half], refs[half:]):
        given[...] = taken[...]


def local(queries, resp_kv, prefix_kv, upstream, gains, rewards, lengths):
    prompts, responses = lax.axis_size("prompt"), lax.axis_size("resp")
    chips, planes = responses // 2, prompts // 2
    gain_slots = 2 + 2 * chips + planes + 1
    arrays = queries, resp_kv, prefix_kv, upstream, gains
    hbm = pl.BlockSpec(memory_space=pltpu.HBM)
    vmem = pl.BlockSpec(memory_space=pltpu.VMEM)
    smem = pl.BlockSpec(memory_space=pltpu.SMEM)
    dma = pltpu.SemaphoreType.DMA
    shapes = (
        jax.ShapeDtypeStruct((ROWS, QUERIES), F32),
        jax.ShapeDtypeStruct((ROWS, 2 * HEAD), F32),
        jax.ShapeDtypeStruct((ROWS, 2 * HEAD), F32),
        jax.ShapeDtypeStruct((2, HEAD), F32),
    )
    found = pl.pallas_call(
        functools.partial(kernel, (prompts, responses)),
        out_shape=tuple(pltpu.VMEM(shape.shape, shape.dtype) for shape in shapes),
        in_specs=[hbm] * 5 + [smem] * 2,
        out_specs=(vmem,) * 4,
        scratch_shapes=[
            pltpu.VMEM((ROWS, QUERIES), BF16),
            pltpu.VMEM((ROWS, QUERIES), BF16),
            pltpu.VMEM((ROWS, 2 * HEAD), BF16),
            pltpu.VMEM((2, HEAD), F32),
            pltpu.VMEM((chips, ROWS, 2 * HEAD), BF16),
            pltpu.VMEM((2, HEAD, QUERIES), BF16),
            pltpu.VMEM((2, HEAD, QUERIES), BF16),
            pltpu.VMEM((2, QUERIES, HEAD), BF16),
            pltpu.VMEM((2, QUERIES, 2 * HEAD), BF16),
            pltpu.VMEM((chips, 2, ROWS, QUERIES), BF16),
            pltpu.VMEM((chips, 2, ROWS, QUERIES), BF16),
            pltpu.VMEM((ROWS, QUERIES), BF16),
            pltpu.VMEM((ROWS, QUERIES), BF16),
            pltpu.VMEM((2, 8, QUERIES), F32),
            pltpu.VMEM((2, 8, QUERIES), F32),
            pltpu.VMEM((2, 8, QUERIES), F32),
            pltpu.VMEM((2, HEAD, QUERIES), F32),
            pltpu.VMEM((2, HEAD, QUERIES), F32),
            pltpu.VMEM((2, 8, QUERIES), F32),
            pltpu.VMEM((2, 8, QUERIES), F32),
            pltpu.VMEM((HEAD, QUERIES), F32),
            pltpu.VMEM((chips + 2, 8, 128), F32),
            pltpu.VMEM((chips, ROWS, 2 * HEAD), BF16),
            pltpu.VMEM((chips, ROWS, 2 * HEAD), BF16),
            pltpu.VMEM((gain_slots, 8, HEAD), F32),
            dma((5,)),
            dma((chips,)),
            dma((chips,)),
            dma((chips,)),
            dma((chips,)),
            dma((chips,)),
            dma((chips,)),
            dma((7,)),
            dma((7,)),
            dma((gain_slots,)),
            dma((gain_slots,)),
        ],
        compiler_params=pltpu.CompilerParams(
            collective_id=0, has_side_effects=True, vmem_limit_bytes=VMEM_LIMIT
        ),
    )(*(pltpu.with_memory_space_constraint(array, pltpu.HBM) for array in arrays), rewards, lengths)
    return pl.pallas_call(
        hand_on,
        out_shape=shapes,
        in_specs=[vmem] * 4,
        out_specs=(vmem,) * 4,
        compiler_params=pltpu.CompilerParams(vmem_limit_bytes=VMEM_LIMIT),
    )(*found)


def solution(mesh):
    rows = P(("prompt", "resp"), None)
    return jax.shard_map(
        local,
        mesh=mesh,
        in_specs=(rows, rows, rows, rows, P(), P("prompt", "resp"), P("prompt")),
        out_specs=(rows, rows, rows, P()),
        check_vma=False,
    )
```

```python
import functools
import math

import jax
import jax.numpy as jnp
from jax import lax
from jax.experimental import pallas as pl
from jax.experimental.pallas import tpu as pltpu
from jax.sharding import PartitionSpec as P

HEAD = 128
HEADS = 8
ROWS = 128
QUERIES = HEADS * ROWS
CHUNK = 256
VMEM_LIMIT = 40 * 1024 * 1024
EPS = 1e-06
SCALE = HEAD ** (-0.5)
EXP2 = SCALE * math.log2(math.e)
MESH = pl.DeviceIdType.MESH
F32 = jnp.float32
BF16 = jnp.bfloat16


def unit_scale(values):
    inverse = lax.rsqrt(jnp.mean(values * values, axis=-1, keepdims=True) + EPS)
    return values * inverse, inverse


def unit_back(grad_normed, unit_values, inverse, gain):
    grad_unit = grad_normed * gain
    inner = jnp.mean(grad_unit * unit_values, axis=-1, keepdims=True)
    return inverse * (grad_unit - unit_values * inner)


def fold(values):
    rows, columns = values.shape
    return jnp.sum(values.reshape(rows // 8, 8, columns), axis=0)


def mm(left, right):
    return lax.dot_general(left, right, (((1,), (0,)), ((), ())), preferred_element_type=F32)


def chunks():
    return [slice(start, start + CHUNK) for start in range(0, QUERIES, CHUNK)]


def offset(slot):
    if isinstance(slot, int):
        return slot * 3 % 8 // 2 % 4, 2 * slot * (slot - 1) % 11 % 2
    return lax.rem(lax.div(lax.rem(slot * 3, 8), 2), 4), lax.rem(lax.rem(2 * slot * (slot - 1), 11), 2)


def mirror(slot):
    along, across = offset(slot)
    return next(other for other in range(8) if offset(other) == ((4 - along) % 4, across))


def heads():
    return [slice(h * HEAD, (h + 1) * HEAD) for h in range(HEADS)]


def kernel(
    sizes,
    queries,
    resp_kv,
    prefix_kv,
    upstream,
    gains,
    rewards,
    lengths,
    grad_query,
    grad_response,
    grad_prefix,
    gain_grads,
    q_in,
    u_in,
    r_in,
    g_in,
    kv,
    q_t,
    u_t,
    key_rows,
    value_rows,
    weights,
    marks,
    self_weights,
    self_marks,
    den_sum,
    mark_sum,
    base,
    mark_grads,
    weight_grads,
    stat_out,
    stat_in,
    grad_in,
    reward_in,
    part_out,
    part_in,
    gain_buf,
    in_sem,
    ag_send,
    ag_recv,
    reward_send,
    reward_recv,
    part_send,
    part_recv,
    twin_send,
    twin_recv,
    gain_send,
    gain_recv,
):
    prompts, responses = sizes
    chips = responses // 2
    planes = prompts // 2
    prompt = lax.axis_index("prompt")
    resp = lax.axis_index("resp")
    chip = resp // 2
    core = lax.rem(resp, 2)
    low = lax.rem(prompt, 2)

    def place_of(slot):
        along, across = offset(slot)
        return lax.rem(lax.div(chip, 2) + along, chips // 2) * 2 + lax.rem(chip + across, 2)

    def to_chip(slot):
        return (prompt, place_of(slot) * 2 + core)

    sibling = (prompt, resp + 1 - 2 * core)

    def to_plane(step):
        row = lax.rem(low + step // chips, 2)
        return (prompt - low + row, lax.rem(chip + lax.rem(step, chips), chips) * 2 + core)

    def to_z(step):
        return (lax.rem(prompt + 2 * step, prompts), resp)

    barrier = pltpu.get_barrier_semaphore()

    def greet(device):
        pl.semaphore_signal(barrier, inc=1, device_id=device, device_id_type=MESH)

    copies = [
        pltpu.make_async_copy(prefix_kv, kv.at[0], in_sem.at[0]),
        pltpu.make_async_copy(queries, q_in, in_sem.at[1]),
        pltpu.make_async_copy(upstream, u_in, in_sem.at[2]),
        pltpu.make_async_copy(resp_kv, r_in, in_sem.at[3]),
        pltpu.make_async_copy(gains, g_in, in_sem.at[4]),
    ]
    for copy in copies:
        copy.start()

    @pl.loop(1, planes)
    def _(step):
        greet(to_z(step))

    @pl.loop(1, 2 * chips)
    def _(step):
        greet(to_plane(step))

    greet(sibling)

    copies[0].wait()
    pl.semaphore_wait(barrier, 1 + (2 * chips - 1) + (planes - 1))

    def remote(src, dst, send, recv, device):
        return pltpu.make_async_remote_copy(
            src_ref=src, dst_ref=dst, send_sem=send, recv_sem=recv, device_id=device, device_id_type=MESH
        )

    def gather(slot):
        return remote(kv.at[0], kv.at[mirror(slot)], ag_send.at[slot], ag_recv.at[mirror(slot)], to_chip(slot))

    def arrival(slot):
        return remote(kv.at[0], kv.at[slot], ag_send.at[slot], ag_recv.at[slot], sibling)

    def twin(place, src, dst):
        return remote(src, dst, twin_send.at[place], twin_recv.at[place], sibling)

    def reward_copy(slot):
        return remote(
            reward_in.at[0],
            reward_in.at[mirror(slot)],
            reward_send.at[slot],
            reward_recv.at[mirror(slot)],
            to_chip(slot),
        )

    for slot in (1, 2, 3):
        gather(slot).start()
    for copy in copies[1:]:
        copy.wait()
    own_reward = rewards[0, 0].astype(F32)
    reward_in[chips] = jnp.full((8, 128), own_reward, F32)
    send_reward = twin(3, reward_in.at[chips], reward_in.at[chips + 1])
    send_reward.start()

    gain_query = g_in[0:1, :]
    gain_key = g_in[1:2, :]
    length = lengths[0]

    row = lax.broadcasted_iota(jnp.int32, (8, 128), 0)
    for h, part in enumerate(heads()):
        for slot in {0: (4,), 2: (5, 6), 4: (7,)}.get(h, ()):
            gather(slot).start()
        if h == 4:
            send_reward.wait_recv()
            pair = reward_in[chips], reward_in[chips + 1]
            reward_in[0] = jnp.where(row == 0, pair[0] + pair[1], pair[0] * pair[0] + pair[1] * pair[1])
            for slot in range(1, chips):
                reward_copy(slot).start()
        unit, _ = unit_scale(q_in[:, part].astype(F32))
        q_t[0, :, part] = jnp.transpose((unit * gain_query).astype(BF16))
        u_t[0, :, part] = jnp.transpose(u_in[:, part])
    send_q = twin(0, q_t.at[0], q_t.at[1])
    send_u = twin(1, u_t.at[0], u_t.at[1])
    send_q.start()
    send_u.start()
    mark_grads[...] = jnp.zeros_like(mark_grads)
    weight_grads[...] = jnp.zeros_like(weight_grads)
    den_sum[1] = jnp.zeros_like(den_sum[1])
    mark_sum[1] = jnp.zeros_like(mark_sum[1])

    def half_of(rows):
        unit, _ = unit_scale(rows.astype(F32))
        return (unit * gain_key).astype(BF16)

    def scores_of(half, rows, side, part, seen):
        weight = jnp.where(seen, jnp.exp2(mm(half, q_t[side, :, part]) * EXP2), 0.0)
        return weight, mm(rows, u_t[side, :, part])

    def visible(step):
        owner = place_of(step) * 2 + core
        return lax.broadcasted_iota(jnp.int32, (ROWS, CHUNK), 0) + owner * ROWS < length

    key_place = lax.broadcasted_iota(jnp.int32, (ROWS, CHUNK), 0)
    token = lax.rem(lax.broadcasted_iota(jnp.int32, (ROWS, CHUNK), 1), ROWS)
    first_keys = [half_of(r_in[:, :HEAD]), half_of(kv[0, :, :HEAD])]
    first_values = [r_in[:, HEAD:], kv[0, :, HEAD:]]
    first_seen = [key_place <= token, visible(0)]
    first_weights = [self_weights, weights.at[0, 0]]
    first_marks = [self_marks, marks.at[0, 0]]
    for part in chunks():
        found = [
            scores_of(half, rows, 0, part, seen) for half, rows, seen in zip(first_keys, first_values, first_seen)
        ]
        den = fold(found[0][0]) + fold(found[1][0])
        mean = jnp.sum(fold(found[0][0] * found[0][1]) + fold(found[1][0] * found[1][1]), axis=0, keepdims=True)
        mean = mean / jnp.sum(den, axis=0, keepdims=True)
        base[0, :, part] = jnp.broadcast_to(mean, den.shape)
        den_sum[0, :, part] = den
        mark_total = jnp.zeros_like(den)
        for (weight, probe), weight_ref, mark_ref in zip(found, first_weights, first_marks):
            mark = weight * (probe - mean)
            mark_total += fold(mark)
            weight_ref[:, part] = weight.astype(BF16)
            mark_ref[:, part] = mark.astype(BF16)
        mark_sum[0, :, part] = mark_total
    send_base = twin(2, base.at[0], base.at[1])
    send_base.start()

    first_t = jnp.transpose(jnp.concatenate(first_keys, axis=0))
    for part in chunks():
        mark_grads[0, :, part] += mm(first_t, jnp.concatenate([ref[:, part] for ref in first_marks], axis=0))
        weight_grads[0, :, part] += mm(first_t, jnp.concatenate([ref[:, part] for ref in first_weights], axis=0))

    def forward(step, sides):
        half = half_of(kv[step, :, :HEAD])
        half_t = jnp.transpose(half)
        seen = visible(step)
        for side in sides:
            for part in chunks():
                weight, probe = scores_of(half, kv[step, :, HEAD:], side, part, seen)
                mark = weight * (probe - base[side, 0:1, part])
                den_sum[side, :, part] += fold(weight)
                mark_sum[side, :, part] += fold(mark)
                weights[step, side, :, part] = weight.astype(BF16)
                marks[step, side, :, part] = mark.astype(BF16)
        for side in sides:
            for part in chunks():
                mark_grads[side, :, part] += mm(half_t, marks[step, side, :, part])
                weight_grads[side, :, part] += mm(half_t, weights[step, side, :, part])

    send_q.wait_recv()
    send_u.wait_recv()
    send_base.wait_recv()
    forward(0, [1])

    @pl.loop(1, chips)
    def _(step):
        arrival(step).wait_recv()
        forward(step, [0, 1])

    for side in range(2):
        den = jnp.sum(den_sum[side], axis=0, keepdims=True)
        total = jnp.sum(mark_sum[side], axis=0, keepdims=True)
        place = lax.broadcasted_iota(jnp.int32, (8, QUERIES), 0)
        stat_out[side] = jnp.where(place == 0, den, total)
    send_stat = twin(4, stat_out, stat_in)
    send_stat.start()

    total = reward_in[0]
    for step in range(1, chips):
        reward_copy(mirror(step)).wait_recv()
        total = total + reward_in[step]
    group = float(responses)
    reward_total, squares = total[0:1, 0:1], total[1:2, 0:1]
    spread = jnp.sqrt(group * squares - reward_total * reward_total) / group
    advantages = [
        (reward_in[chips + side, 0:1, 0:1] - reward_total / group) / jnp.maximum(spread, 1.0) for side in range(2)
    ]

    send_stat.wait_recv()
    inverse_den, delta, value_factor, key_factor = [], [], [], []
    for side in range(2):
        both = stat_out[side] + stat_in[1 - side]
        inverse_den.append(1.0 / both[0:1, :])
        delta.append(both[1:2, :] * inverse_den[side])
        value_factor.append(inverse_den[side] * advantages[side])
        key_factor.append(value_factor[side] * SCALE)

    plane_base = 2
    z_base = plane_base + 2 * chips
    z_own = z_base + planes

    def gain_plane(step):
        back = lax.rem(chips - lax.rem(step, chips), chips) + (step // chips) * chips
        return remote(
            gain_buf.at[plane_base],
            gain_buf.at[plane_base + back],
            gain_send.at[plane_base + step],
            gain_recv.at[plane_base + back],
            to_plane(step),
        )

    def gain_z(step):
        return remote(
            gain_buf.at[z_own],
            gain_buf.at[z_base + planes - step],
            gain_send.at[z_base + step],
            gain_recv.at[z_base + planes - step],
            to_z(step),
        )

    query_total = jnp.zeros((HEAD, ROWS), F32)
    for side in range(2):
        for part in heads():
            grad_t = mark_grads[side, :, part] - weight_grads[side, :, part] * delta[side][:, part]
            grad_t = grad_t * key_factor[side][:, part]
            mark_grads[side, :, part] = grad_t
            query_total += grad_t * q_t[side, :, part].astype(F32)
    shared = jnp.sum(fold(jnp.transpose(query_total)), axis=0, keepdims=True)
    gain_buf[z_own] = jnp.where(row == 0, shared / gain_query, jnp.where(row == 1, shared / gain_key, 0.0))

    for step in sorted(range(1, planes), key=lambda step: abs(step - planes // 2)):
        gain_z(step).start()

    send_grad = twin(5, mark_grads.at[1], grad_in)
    send_grad.start()

    for side in range(2):
        for part in heads():
            scaled = q_t[side, :, part].astype(F32) * key_factor[side][:, part]
            raised = u_t[side, :, part].astype(F32) * value_factor[side][:, part]
            key_rows[side, part, :] = jnp.transpose(scaled.astype(BF16))
            value_rows[side, part, :HEAD] = jnp.transpose((scaled * -delta[side][:, part]).astype(BF16))
            value_rows[side, part, HEAD:] = jnp.transpose(raised.astype(BF16))

    def part_copy(step):
        return remote(
            part_out.at[step], part_in.at[mirror(step)], part_send.at[step], part_recv.at[mirror(step)], to_chip(step)
        )

    def key_grads(weight, mark, side):
        both = mm(weight, value_rows[side])
        return both[:, :HEAD] + mm(mark, key_rows[side]), both[:, HEAD:]

    def backward(first, count):
        sums = [
            key_grads(
                weights[first : first + count, side].reshape(count * ROWS, QUERIES),
                marks[first : first + count, side].reshape(count * ROWS, QUERIES),
                side,
            )
            for side in range(2)
        ]
        grad_key, grad_value = sums[0][0] + sums[1][0], sums[0][1] + sums[1][1]
        for at in reversed(range(count)):
            rows = slice(at * ROWS, (at + 1) * ROWS)
            if first + at:
                part_out[first + at, :, :HEAD] = grad_key[rows].astype(BF16)
                part_out[first + at, :, HEAD:] = grad_value[rows].astype(BF16)
                part_copy(first + at).start()
        return grad_key[:ROWS], grad_value[:ROWS]

    quarter = chips // 4
    backward(3 * quarter, quarter)
    backward(2 * quarter, quarter)
    sum_key, sum_value = backward(0, 2 * quarter)
    self_key, self_value = key_grads(self_weights[...], self_marks[...], 0)

    unit, inverse = unit_scale(r_in[:, :HEAD].astype(F32))
    grad_response[:, :HEAD] = unit_back(self_key, unit, inverse, gain_key)
    grad_response[:, HEAD:] = self_value
    send_grad.wait_recv()
    for part in heads():
        grad_normed = jnp.transpose(mark_grads[0, :, part] + grad_in[:, part])
        unit, inverse = unit_scale(q_in[:, part].astype(F32))
        grad_query[:, part] = unit_back(grad_normed, unit, inverse, gain_query)
    @pl.loop(1, planes)
    def _(step):
        gain_z(step).wait_recv()

    total = gain_buf[z_own]
    for step in range(1, planes):
        total = total + gain_buf[z_base + step]
    gain_buf[0] = total
    send_gain = twin(6, gain_buf.at[0], gain_buf.at[1])
    send_gain.start()
    send_gain.wait_recv()
    gain_buf[plane_base] = gain_buf[0] + gain_buf[1]

    for step in sorted(range(1, 2 * chips), key=lambda step: abs(step % chips - chips // 2)):
        gain_plane(step).start()

    for step in range(1, chips):
        part_copy(mirror(step)).wait_recv()
        sum_key += part_in[step, :, :HEAD].astype(F32)
        sum_value += part_in[step, :, HEAD:].astype(F32)
    unit, inverse = unit_scale(kv[0, :, :HEAD].astype(F32))
    grad_prefix[:, :HEAD] = unit_back(sum_key, unit, inverse, gain_key)
    grad_prefix[:, HEAD:] = sum_value

    for copy in (send_q, send_u, send_base, send_reward, send_stat, send_grad, send_gain):
        copy.wait_send()

    for step in range(1, chips):
        gather(step).wait_send()
        reward_copy(step).wait_send()
        part_copy(step).wait_send()

    @pl.loop(1, planes)
    def _(step):
        gain_z(step).wait_send()

    @pl.loop(1, 2 * chips)
    def _(step):
        gain_plane(step).wait_recv()

    total = gain_buf[plane_base]
    for step in range(1, 2 * chips):
        total = total + gain_buf[plane_base + step]
    gain_grads[...] = total[0:2, :] / math.sqrt(prompts * responses * ROWS)

    @pl.loop(1, 2 * chips)
    def _(step):
        gain_plane(step).wait_send()


def hand_on(*refs):
    half = len(refs) // 2
    for taken, given in zip(refs[:half], refs[half:]):
        given[...] = taken[...]


def local(queries, resp_kv, prefix_kv, upstream, gains, rewards, lengths):
    prompts, responses = lax.axis_size("prompt"), lax.axis_size("resp")
    chips, planes = responses // 2, prompts // 2
    gain_slots = 2 + 2 * chips + planes + 1
    arrays = queries, resp_kv, prefix_kv, upstream, gains
    hbm = pl.BlockSpec(memory_space=pltpu.HBM)
    vmem = pl.BlockSpec(memory_space=pltpu.VMEM)
    smem = pl.BlockSpec(memory_space=pltpu.SMEM)
    dma = pltpu.SemaphoreType.DMA
    shapes = (
        jax.ShapeDtypeStruct((ROWS, QUERIES), F32),
        jax.ShapeDtypeStruct((ROWS, 2 * HEAD), F32),
        jax.ShapeDtypeStruct((ROWS, 2 * HEAD), F32),
        jax.ShapeDtypeStruct((2, HEAD), F32),
    )
    found = pl.pallas_call(
        functools.partial(kernel, (prompts, responses)),
        out_shape=tuple(pltpu.VMEM(shape.shape, shape.dtype) for shape in shapes),
        in_specs=[hbm] * 5 + [smem] * 2,
        out_specs=(vmem,) * 4,
        scratch_shapes=[
            pltpu.VMEM((ROWS, QUERIES), BF16),
            pltpu.VMEM((ROWS, QUERIES), BF16),
            pltpu.VMEM((ROWS, 2 * HEAD), BF16),
            pltpu.VMEM((2, HEAD), F32),
            pltpu.VMEM((chips, ROWS, 2 * HEAD), BF16),
            pltpu.VMEM((2, HEAD, QUERIES), BF16),
            pltpu.VMEM((2, HEAD, QUERIES), BF16),
            pltpu.VMEM((2, QUERIES, HEAD), BF16),
            pltpu.VMEM((2, QUERIES, 2 * HEAD), BF16),
            pltpu.VMEM((chips, 2, ROWS, QUERIES), BF16),
            pltpu.VMEM((chips, 2, ROWS, QUERIES), BF16),
            pltpu.VMEM((ROWS, QUERIES), BF16),
            pltpu.VMEM((ROWS, QUERIES), BF16),
            pltpu.VMEM((2, 8, QUERIES), F32),
            pltpu.VMEM((2, 8, QUERIES), F32),
            pltpu.VMEM((2, 8, QUERIES), F32),
            pltpu.VMEM((2, HEAD, QUERIES), F32),
            pltpu.VMEM((2, HEAD, QUERIES), F32),
            pltpu.VMEM((2, 8, QUERIES), F32),
            pltpu.VMEM((2, 8, QUERIES), F32),
            pltpu.VMEM((HEAD, QUERIES), F32),
            pltpu.VMEM((chips + 2, 8, 128), F32),
            pltpu.VMEM((chips, ROWS, 2 * HEAD), BF16),
            pltpu.VMEM((chips, ROWS, 2 * HEAD), BF16),
            pltpu.VMEM((gain_slots, 8, HEAD), F32),
            dma((5,)),
            dma((chips,)),
            dma((chips,)),
            dma((chips,)),
            dma((chips,)),
            dma((chips,)),
            dma((chips,)),
            dma((7,)),
            dma((7,)),
            dma((gain_slots,)),
            dma((gain_slots,)),
        ],
        compiler_params=pltpu.CompilerParams(
            collective_id=0, has_side_effects=True, vmem_limit_bytes=VMEM_LIMIT
        ),
    )(*(pltpu.with_memory_space_constraint(array, pltpu.HBM) for array in arrays), rewards, lengths)
    return pl.pallas_call(
        hand_on,
        out_shape=shapes,
        in_specs=[vmem] * 4,
        out_specs=(vmem,) * 4,
        compiler_params=pltpu.CompilerParams(vmem_limit_bytes=VMEM_LIMIT),
    )(*found)


def solution(mesh):
    rows = P(("prompt", "resp"), None)
    return jax.shard_map(
        local,
        mesh=mesh,
        in_specs=(rows, rows, rows, rows, P(), P("prompt", "resp"), P("prompt")),
        out_specs=(rows, rows, rows, P()),
        check_vma=False,
    )
```
